256 devices in a mesh: vseq: 64 (over y, x, z_hi), aseq: 4 (over z_lo, core).
Axes of the slice: x: 4, y: 4, z: 8 (z_hi: 4, z_lo: 2; z = z_hi * 2 + z_lo), core: 2. Of those that a mesh axis runs over, the one named last changes fastest.
Arguments:
- video_query: bfloat16 [32768, 3072], P('vseq', 'aseq'), may hold values from -40 to 40
- audio_key: bfloat16 [8192, 3072], P('vseq', 'aseq'), may hold values from -40 to 40
- audio_value: bfloat16 [8192, 3072], P('vseq', 'aseq'), may hold values from -6 to 6
- window_first: int32 [256], P('vseq'), may hold values from 0 to 252, as said below
- window_count: int32 [256], P('vseq'), may hold values from 4 to 20
- out_weight: bfloat16 [3072, 3072], P(None, 'aseq'), may hold values from -0.109375 to 0.109375
- cotangent: bfloat16 [32768, 3072], P('vseq', 'aseq'), may hold values from -16 to 16
Outputs:
- mixed_video: bfloat16 [32768, 3072], P('vseq', 'aseq')
- grad_query: float32 [32768, 3072], P('vseq', 'aseq')
- grad_key: float32 [8192, 3072], P('vseq', 'aseq')
- grad_value: float32 [8192, 3072], P('vseq', 'aseq')
- grad_weight: float32 [3072, 3072], P('vseq', 'aseq')
The draws below stay inside these ranges and needn't reach their ends.
Inputs may be any that keep to these rules, and one draw needn't show every extreme that they name: `window_first`: the window of a video block in shard s of vseq (tokens s * 512 onward) starts at or after audio block (s - 2) * (4) and at or before s * 4, and ends at or after (s + 1) * (4) and at or before (s + 3) * 4, inside the audio sequence.
All inputs are finite; a program needn't handle non-finite values.
Results may differ from the reference program's by a relative error of at most 0.023.
Values may be sent and summed in bfloat16 or wider, within the bound.
No kernel may reach another device: no remote copies, remote signals or barrier semaphores. Data moves between devices by JAX's collectives and lax.ppermute only.
A program may use at most 128 MiB of HBM per device.

```python
import math
import jax
import jax.numpy as jnp
from jax import lax

D = 3072
HEAD = 128
TV_DEV = 512
TA_DEV = 128
VBLK = 128
ABLK = 32
REACH = 2
LV = 32768
LA = 8192
N_VSEQ = 64


def window_table(key):
    video_blocks = TV_DEV // VBLK
    per_shard = TA_DEV // ABLK
    total = TV_DEV * N_VSEQ // VBLK
    audio_total = TA_DEV * N_VSEQ // ABLK
    index = jnp.arange(total, dtype=jnp.int32)
    owner = index // video_blocks
    lower = jax.random.randint(jax.random.fold_in(key, 21), (total,), 0, REACH * per_shard + 1, jnp.int32)
    upper = jax.random.randint(jax.random.fold_in(key, 22), (total,), 0, REACH * per_shard + 1, jnp.int32)
    first = jnp.maximum(owner * per_shard - lower, 0)
    last = jnp.minimum((owner + 1) * per_shard + upper, audio_total)
    middle = total // 2
    wide_owner = middle // video_blocks
    first = first.at[middle].set((wide_owner - REACH) * per_shard)
    last = last.at[middle].set((wide_owner + 1 + REACH) * per_shard)
    first = first.at[1].set(0)
    last = last.at[1].set(per_shard)
    first = first.at[total - 1].set((N_VSEQ - 1) * per_shard)
    last = last.at[total - 1].set(audio_total)
    return (first, last - first)


def draw_window_first(key, part):
    table = window_table(key)
    return table[0].astype(jnp.int32)


def draw_window_count(key, part):
    table = window_table(key)
    return table[1].astype(jnp.int32)


def draw_video_query(key, part):
    key = jax.random.fold_in(key, 11)
    total_rows = TV_DEV * N_VSEQ
    values = jnp.clip(jax.random.normal(key, (total_rows, D), jnp.float32), -5.0, 5.0)
    return values.astype(jnp.bfloat16)


def draw_audio_key(key, part):
    key = jax.random.fold_in(key, 13)
    total_rows = TA_DEV * N_VSEQ
    values = jnp.clip(jax.random.normal(key, (total_rows, D), jnp.float32), -5.0, 5.0)
    return values.astype(jnp.bfloat16)


def raised(entries, own_key, source, target, shards_of, factor):
    def block_of(axis_at):
        return (jnp.arange(entries.shape[axis_at]) // (entries.shape[axis_at] // shards_of)).reshape((-1,) + (1,) * (entries.ndim - 1 - axis_at))

    first = jax.random.permutation(own_key, shards_of)[block_of(target)]
    other_side = (block_of(target) + shards_of // 2) % shards_of
    return jnp.where((block_of(source) == first) | (block_of(source) == other_side), factor * entries, entries)


def level_of(key, extent, split, smallest, high):
    factor_of = 1.0
    for dim, shards_of in split:
        steps = jax.random.uniform(jax.random.fold_in(jax.random.fold_in(key, 6), dim), (shards_of,), jnp.float32, smallest / len(split), high / len(split))
        factor_of = factor_of * jnp.repeat(jnp.exp(steps), extent[dim] // shards_of).reshape((-1,) + (1,) * (len(extent) - 1 - dim))
    return factor_of


def scatter_about(stream_key, extent, deviation, reach, split=(), kind=jnp.bfloat16):
    drawn = deviation * jax.random.normal(stream_key, extent, jnp.float32)
    if split:
        drawn = drawn * level_of(stream_key, extent, split, -0.22, 0.18)
    return jnp.clip(drawn, -reach, reach).astype(kind)


def noise_with(stream_key, extent, scale, limit, split, heavy, held_as=jnp.bfloat16):
    drawn = scale * jax.random.normal(stream_key, extent, jnp.float32)
    if split:
        drawn = drawn * level_of(stream_key, extent, split, -0.22, 0.18)
    return jnp.clip(raised(drawn, jax.random.fold_in(stream_key, 3), *heavy), -limit, limit).astype(held_as)


def setup_inputs(seed: int = 0) -> dict:
    key_of = jax.random.split(jax.random.key(seed), 8)
    return {
        "video_query": draw_video_query(jax.random.fold_in(key_of[7], 71), 0),
        "audio_key": draw_audio_key(jax.random.fold_in(key_of[7], 71), 0),
        "audio_value": scatter_about(key_of[2], (LA, D), 1.0, 6.0, ((0, 64), (1, 4))),
        "window_first": draw_window_first(jax.random.fold_in(key_of[7], 71), 0),
        "window_count": draw_window_count(jax.random.fold_in(key_of[7], 71), 0),
        "out_weight": scatter_about(key_of[5], (D, D), D ** -0.5, 0.109375, ((1, 4),)),
        "cotangent": noise_with(key_of[6], (LV, D), 1.0, 16.0, ((0, 64), (1, 4)), (0, 1, 64, 4.0)),
    }


def reference(video_query, audio_key, audio_value, window_first, window_count, out_weight, cotangent):
    feature = video_query.shape[1]
    head_count = feature // HEAD
    score_scale = 1.0 / math.sqrt(HEAD)
    band_rows = (2 * REACH + 1) * TA_DEV
    per_shard = TA_DEV // ABLK
    video_blocks = TV_DEV // VBLK
    margin = jnp.zeros((REACH * TA_DEV, feature), jnp.bfloat16)
    padded_key = jnp.concatenate([margin, audio_key, margin], axis=0)
    padded_value = jnp.concatenate([margin, audio_value, margin], axis=0)
    grad_attn = jnp.dot(cotangent, out_weight, preferred_element_type=jnp.float32).astype(jnp.bfloat16)

    def shard_step(carry, position):
        query = lax.dynamic_slice_in_dim(video_query, position * TV_DEV, TV_DEV, 0)
        band_key = lax.dynamic_slice_in_dim(padded_key, position * TA_DEV, band_rows, 0)
        band_value = lax.dynamic_slice_in_dim(padded_value, position * TA_DEV, band_rows, 0)
        grad_rows = lax.dynamic_slice_in_dim(grad_attn, position * TV_DEV, TV_DEV, 0)
        first = lax.dynamic_slice_in_dim(window_first, position * video_blocks, video_blocks, 0)
        count = lax.dynamic_slice_in_dim(window_count, position * video_blocks, video_blocks, 0)
        row_first = jnp.broadcast_to(first[:, None], (video_blocks, VBLK)).reshape(TV_DEV)
        row_end = jnp.broadcast_to((first + count)[:, None], (video_blocks, VBLK)).reshape(TV_DEV)
        key_block = (position - REACH) * per_shard + jnp.arange(band_rows, dtype=jnp.int32) // ABLK
        allowed = (key_block[None, :] >= row_first[:, None]) & (key_block[None, :] < row_end[:, None])
        query_heads = query.reshape(TV_DEV, head_count, HEAD).astype(jnp.float32)
        key_heads = band_key.reshape(band_rows, head_count, HEAD).astype(jnp.float32)
        value_heads = band_value.reshape(band_rows, head_count, HEAD).astype(jnp.float32)
        grad_heads = grad_rows.reshape(TV_DEV, head_count, HEAD)
        scores = jnp.einsum('thd,khd->htk', query_heads, key_heads) * score_scale
        masked = jnp.where(allowed[None], scores, -jnp.inf)
        exponent = jnp.exp(masked - lax.optimization_barrier(jnp.max(masked, axis=-1, keepdims=True)))
        probs_full = exponent / lax.optimization_barrier(jnp.sum(exponent, axis=-1, keepdims=True))
        probs_half = probs_full.astype(jnp.bfloat16)
        attended = jnp.einsum('htk,khd->thd', probs_half.astype(jnp.float32), value_heads).astype(jnp.bfloat16)
        row_delta = lax.optimization_barrier(jnp.sum(grad_heads.astype(jnp.float32) * attended.astype(jnp.float32), axis=-1))
        prob_grad = jnp.einsum('thd,khd->htk', grad_heads.astype(jnp.float32), value_heads)
        score_grad = (probs_full * (prob_grad - jnp.transpose(row_delta)[:, :, None])).astype(jnp.bfloat16)
        grad_query = jnp.einsum('htk,khd->thd', score_grad.astype(jnp.float32), key_heads) * score_scale
        band_key_grad = jnp.einsum('htk,thd->khd', score_grad.astype(jnp.float32), query_heads) * score_scale
        band_value_grad = jnp.einsum('htk,thd->khd', probs_half.astype(jnp.float32), grad_heads.astype(jnp.float32))
        band_grad = jnp.stack([band_key_grad.reshape(band_rows, feature), band_value_grad.reshape(band_rows, feature)])
        start = position * TA_DEV
        current = lax.dynamic_slice_in_dim(carry, start, band_rows, 1)
        carry = lax.dynamic_update_slice_in_dim(carry, current + band_grad, start, 1)
        return (carry, (attended.reshape(TV_DEV, feature), grad_query.reshape(TV_DEV, feature)))
    initial = jnp.zeros((2, (N_VSEQ + 2 * REACH) * TA_DEV, feature), jnp.float32)
    positions = jnp.arange(N_VSEQ, dtype=jnp.int32)
    summed, (attended_all, grad_query_all) = lax.scan(shard_step, initial, positions)
    attended_flat = attended_all.reshape(N_VSEQ * TV_DEV, feature)
    mixed_video = jnp.dot(attended_flat, out_weight.T, preferred_element_type=jnp.float32).astype(jnp.bfloat16)
    grad_weight = jnp.dot(cotangent.T, attended_flat, preferred_element_type=jnp.float32)
    inner = summed[:, REACH * TA_DEV:(REACH + N_VSEQ) * TA_DEV]
    grad_query = grad_query_all.reshape(N_VSEQ * TV_DEV, feature)
    return (mixed_video, grad_query, inner[0], inner[1], grad_weight)
```

```python
import functools
import math

import jax
import jax.numpy as jnp
from jax import lax
from jax.experimental import pallas as pl
from jax.experimental.pallas import tpu as pltpu
from jax.sharding import PartitionSpec as P

HEAD = 128
VBLK = 128
ABLK = 32
RING = 4
SCALE = 1.0 / math.sqrt(HEAD)
LOG2E = math.log2(math.e)
NT = (((1,), (1,)), ((), ()))
TN = (((0,), (0,)), ((), ()))
NN = (((1,), (0,)), ((), ()))
F32 = jnp.float32
BF = jnp.bfloat16
CORE = [(a, a ^ 1) for a in range(4)]
PAIR = [(a, a ^ 2) for a in range(4)]


def dot(a, b, dims):
    return lax.dot_general(a, b, dims, preferred_element_type=F32)


def attend_forward(q_ref, k0, k1, k2, k3, k4, bias_ref, att_ref, p_ref):
    pieces = (k0, k1, k2, k3, k4)
    q = q_ref[...]
    tokens = q.shape[0]
    rows = k0.shape[1]
    blocks = rows // ABLK
    scores = []
    for i, kv in enumerate(pieces):
        tile = dot(kv[0], q, NT).reshape(blocks, ABLK, tokens)
        tile = tile + bias_ref[blocks * i : blocks * (i + 1), :][:, None, :]
        scores.append(tile.reshape(rows, tokens))
    top = jnp.max(functools.reduce(jnp.maximum, scores), axis=0, keepdims=True)
    exponent = [jnp.exp2((tile - top) * (SCALE * LOG2E)) for tile in scores]
    total = jnp.sum(functools.reduce(jnp.add, exponent), axis=0, keepdims=True)
    share = 1.0 / total
    for i, tile in enumerate(exponent):
        p_ref[0, rows * i : rows * (i + 1), :] = (tile * share).astype(BF)
    values = jnp.concatenate([kv[1] for kv in pieces], axis=0)
    att_ref[...] = dot(values, p_ref[0], TN).T.astype(BF)


def attend_backward(
    q_ref, k0, k1, k2, k3, k4, p_ref, att_ref, do_ref, dq_ref, g0, g1, g2, g3, g4
):
    pieces = (k0, k1, k2, k3, k4)
    grads = (g0, g1, g2, g3, g4)
    q = q_ref[...]
    do = do_ref[...]
    rows = k0.shape[1]
    do_t = do.T
    delta = jnp.sum(
        do_t.astype(F32) * att_ref[...].T.astype(F32), axis=0, keepdims=True
    )
    score_grads = []
    for i, kv in enumerate(pieces):
        p = p_ref[0, rows * i : rows * (i + 1), :]
        prob_grad = dot(kv[1], do_t, NN)
        ds = (p.astype(F32) * (prob_grad - delta)).astype(BF)
        score_grads.append(ds)
        grads[i][0] = (dot(ds, q, NN) * SCALE).astype(grads[i].dtype)
        grads[i][1] = dot(p, do, NN).astype(grads[i].dtype)
    keys = jnp.concatenate([kv[0] for kv in pieces], axis=0)
    dq_ref[...] = (dot(keys, jnp.concatenate(score_grads, axis=0), TN) * SCALE).T


def forward_call(q, pieces, bias):
    tokens, feature = q.shape
    heads = feature // HEAD
    rows = pieces[0].shape[1]
    band = rows * len(pieces)
    by_head = pl.BlockSpec((tokens, HEAD), lambda h: (0, h))
    kv_head = pl.BlockSpec((2, rows, HEAD), lambda h: (0, 0, h))
    return pl.pallas_call(
        attend_forward,
        grid=(heads,),
        in_specs=[by_head] + [kv_head] * 5 + [pl.BlockSpec(bias.shape, lambda h: (0, 0))],
        out_specs=[by_head, pl.BlockSpec((1, band, tokens), lambda h: (h, 0, 0))],
        out_shape=[
            jax.ShapeDtypeStruct((tokens, feature), BF),
            jax.ShapeDtypeStruct((heads, band, tokens), BF),
        ],
        compiler_params=pltpu.CompilerParams(vmem_limit_bytes=40 << 20),
        cost_estimate=pl.CostEstimate(
            flops=4 * tokens * band * feature,
            bytes_accessed=heads * band * tokens * 2 + 2 * tokens * feature * 2,
            transcendentals=heads * band * tokens,
        ),
        name="attend_forward",
    )(q, *pieces, bias)


def backward_call(q, pieces, p, att, do):
    tokens, feature = q.shape
    heads = feature // HEAD
    rows = pieces[0].shape[1]
    band = rows * len(pieces)
    by_head = pl.BlockSpec((tokens, HEAD), lambda h: (0, h))
    kv_head = pl.BlockSpec((2, rows, HEAD), lambda h: (0, 0, h))
    piece = lambda kind: jax.ShapeDtypeStruct((2, rows, feature), kind)
    return pl.pallas_call(
        attend_backward,
        grid=(heads,),
        in_specs=[by_head]
        + [kv_head] * 5
        + [pl.BlockSpec((1, band, tokens), lambda h: (h, 0, 0)), by_head, by_head],
        out_specs=[by_head] + [kv_head] * 5,
        out_shape=[jax.ShapeDtypeStruct((tokens, feature), F32)]
        + [piece(F32), piece(F32), piece(F32), piece(BF), piece(BF)],
        compiler_params=pltpu.CompilerParams(vmem_limit_bytes=40 << 20),
        cost_estimate=pl.CostEstimate(
            flops=8 * tokens * band * feature,
            bytes_accessed=heads * band * tokens * 2 + tokens * feature * 10,
            transcendentals=0,
        ),
        name="attend_backward",
    )(q, *pieces, p, att, do)


def place(s):
    return s // (RING * RING), (s // RING) % RING, s % RING


def index(y, x, z):
    return (y * RING + x) * RING + z


def odd_swap(i, n):
    return (((i + 1) % n ^ 1) - 1) % n


def at(array, i):
    return lax.dynamic_index_in_dim(array, i, 0, keepdims=False)


def ring_sum(chunk, pos, even, odd):
    halves = lambda v: (v[: v.shape[0] // 2], v[v.shape[0] // 2 :])
    far = halves(chunk((pos + 2) % RING).astype(BF))
    from_even = lax.ppermute(far[0], "vseq", even)
    from_odd = lax.ppermute(far[1], "vseq", odd)
    to_even = halves(chunk(pos ^ 1))
    to_odd = halves(chunk(odd_swap(pos, RING)))
    to_even = jnp.concatenate(
        [to_even[0].astype(BF), (to_even[1].astype(F32) + from_odd.astype(F32)).astype(BF)], 0
    )
    to_odd = jnp.concatenate(
        [(to_odd[0].astype(F32) + from_even.astype(F32)).astype(BF), to_odd[1].astype(BF)], 0
    )
    even_sum = lax.ppermute(to_even, "vseq", even)
    odd_sum = lax.ppermute(to_odd, "vseq", odd)
    return chunk(pos).astype(F32) + even_sum.astype(F32) + odd_sum.astype(F32)


def local(video_query, audio_key, audio_value, window_first, window_count, out_weight, cotangent):
    tokens, feature = video_query.shape
    audio_rows = audio_key.shape[0]
    shards = lax.axis_size("vseq")
    s = lax.axis_index("vseq")
    a = lax.axis_index("aseq")
    y, x, z = place(s)
    each = range(shards)
    pa = [(i, i ^ 1) for i in each]
    pb = [(i, odd_swap(i, shards)) for i in each]

    def along(change):
        return [(i, index(*change(*place(i)))) for i in each]

    x_even = along(lambda y, x, z: (y, x ^ 1, z))
    x_odd = along(lambda y, x, z: (y, odd_swap(x, RING), z))
    y_even = along(lambda y, x, z: (y ^ 1, x, z))
    y_odd = along(lambda y, x, z: (odd_swap(y, RING), x, z))

    kv = jnp.stack([audio_key, audio_value])
    kv_a = lax.ppermute(kv, "vseq", pa)
    kv_b = lax.ppermute(kv, "vseq", pb)
    kv_aa = lax.ppermute(kv_b, "vseq", pa)
    kv_bb = lax.ppermute(kv_a, "vseq", pb)
    pieces = (kv, kv_a, kv_b, kv_aa, kv_bb)

    cot_core = lax.ppermute(cotangent, "aseq", CORE)
    cot_own, _, _ = lax.optimization_barrier((cotangent, kv_a, kv_b))
    cot_pair = lax.ppermute(cot_own, "aseq", PAIR)
    cot_both = lax.ppermute(cot_pair, "aseq", CORE)

    per_shard = audio_rows // ABLK
    step = 1 - 2 * (s % 2)
    offsets = jnp.stack([0 * step, step, -step, 2 * step, -2 * step])
    key_block = ((s + offsets)[:, None] * per_shard + jnp.arange(per_shard)[None, :]).reshape(-1)
    first = jnp.repeat(window_first, VBLK)
    end = jnp.repeat(window_first + window_count, VBLK)
    allowed = (key_block[:, None] >= first[None, :]) & (key_block[:, None] < end[None, :])
    bias = jnp.where(allowed, 0.0, -1e30).astype(F32)

    weight_parts = out_weight.reshape(4, feature, feature)
    weight = [at(weight_parts, a ^ j) for j in range(4)]

    att, p = forward_call(video_query, pieces, bias)

    far_core = dot(att, jnp.concatenate([weight[1], weight[3]], 0), NT).astype(BF)
    got_core = lax.ppermute(far_core, "aseq", CORE).astype(F32)
    far_pair = (dot(att, weight[2], NT) + got_core[:, feature:]).astype(BF)
    got_pair = lax.ppermute(far_pair, "aseq", PAIR).astype(F32)
    mixed_video = (dot(att, weight[0], NT) + got_core[:, :feature] + got_pair).astype(BF)

    cot = jnp.concatenate([cotangent, cot_core, cot_pair, cot_both], axis=1)
    grad_attn = dot(cot, jnp.concatenate(weight, 0), NN).astype(BF)
    grad_query, g_own, g_a, g_b, g_aa, g_bb = backward_call(
        video_query, pieces, p, att, grad_attn
    )

    back_a = lax.ppermute(g_aa, "vseq", pa)
    back_b = lax.ppermute(g_bb, "vseq", pb)
    sum_b = lax.ppermute((g_b + back_a.astype(F32)).astype(BF), "vseq", pb)
    sum_a = lax.ppermute((g_a + back_b.astype(F32)).astype(BF), "vseq", pa)
    grad_kv = g_own + sum_a.astype(F32) + sum_b.astype(F32)

    half = feature // 2
    part = feature // RING
    gw_x = dot(cot, att[:, :half], TN).astype(BF).reshape(RING, RING, part, half)
    gw_y = dot(cot, att[:, half:], TN).astype(BF).reshape(RING, feature, half)
    sum_x = ring_sum(lambda i: lax.dynamic_index_in_dim(gw_x, i, 1, keepdims=False), x, x_even, x_odd)
    sum_y = ring_sum(lambda i: at(gw_y, i ^ a), y, y_even, y_odd)
    sum_xy = ring_sum(lambda i: at(sum_x, i ^ a), y, y_even, y_odd)
    sum_yx = ring_sum(lambda i: at(sum_y.reshape(RING, part, half), i), x, x_even, x_odd)
    plane = jnp.concatenate([sum_xy, sum_yx], axis=1).reshape(RING, part // RING, feature)
    grad_weight = at(plane, z)
    for j in range(1, RING):
        swap = along(lambda y, x, z: (y, x, z ^ j))
        got = lax.ppermute(at(plane, z ^ j).astype(BF), "vseq", swap)
        grad_weight = grad_weight + got.astype(F32)
    return (mixed_video, grad_query, grad_kv[0], grad_kv[1], grad_weight)


def solution(mesh):
    both = P("vseq", "aseq")
    in_specs = (both, both, both, P("vseq"), P("vseq"), P(None, "aseq"), both)
    return jax.shard_map(
        local, mesh=mesh, in_specs=in_specs, out_specs=(both,) * 5, check_vma=False
    )
```

```python
import functools
import math

import jax
import jax.numpy as jnp
import numpy as np
from jax import lax
from jax.experimental import pallas as pl
from jax.experimental.pallas import tpu as pltpu
from jax.sharding import PartitionSpec as P

HEAD = 128
VBLK = 128
ABLK = 32
RING = 4
SCALE = 1.0 / math.sqrt(HEAD)
LOG2E = math.log2(math.e)
NT = (((1,), (1,)), ((), ()))
TN = (((0,), (0,)), ((), ()))
NN = (((1,), (0,)), ((), ()))
F32 = jnp.float32
BF = jnp.bfloat16
VMEM = 32 << 20
CORE = [(a, a ^ 1) for a in range(4)]
PAIR = [(a, a ^ 2) for a in range(4)]


def dot(a, b, dims):
    return lax.dot_general(a, b, dims, preferred_element_type=F32)


def attend_forward(
    pos, q_ref, k0, k1, k2, k3, k4, v0, v1, v2, v3, v4, bias_ref, w_ref, l0, l1,
    att_ref, p_ref, out_ref, gw_ref, far0, far1, all_ref,
):
    q = q_ref[...]
    tokens = q.shape[0]
    rows = k0.shape[0]
    blocks = rows // ABLK
    scores = []
    for i, k in enumerate((k0, k1, k2, k3, k4)):
        tile = dot(k[...], q, NT).reshape(blocks, ABLK, tokens)
        tile = tile + bias_ref[blocks * i : blocks * (i + 1), :][:, None, :]
        scores.append(tile.reshape(rows, tokens))
    top = jnp.max(functools.reduce(jnp.maximum, scores), axis=0, keepdims=True)
    exponent = [jnp.exp2((tile - top) * (SCALE * LOG2E)) for tile in scores]
    total = jnp.sum(functools.reduce(jnp.add, exponent), axis=0, keepdims=True)
    share = 1.0 / total
    for i, tile in enumerate(exponent):
        p_ref[0, rows * i : rows * (i + 1), :] = (tile * share).astype(BF)
    values = jnp.concatenate([v[...] for v in (v0, v1, v2, v3, v4)], axis=0)
    att = dot(values, p_ref[0], TN).T.astype(BF)
    att_ref[...] = att
    head = pl.program_id(0)
    all_ref[:, pl.ds(pl.multiple_of(head * HEAD, HEAD), HEAD)] = att

    @pl.when(head == pl.num_programs(0) - 1)
    def _():
        out_ref[...] = dot(all_ref[...], w_ref[...], NT).astype(BF)
        weight_rows((l0, l1), all_ref, gw_ref)
        far0[...] = gw_ref[0, pos[FAR]]
        far1[...] = gw_ref[1, pos[FAR]]


def weight_rows(lefts, att_ref, gw_ref):
    part = gw_ref.shape[2]
    for j, left in enumerate(lefts):
        rows = dot(left[...], att_ref[...], TN).astype(BF)
        for i in range(RING):
            gw_ref[j, i] = rows[i * part : (i + 1) * part]


def attend_backward(
    given, q_ref, k0, k1, k2, k3, k4, v0, v1, v2, v3, v4, p_ref, att_ref, near_ref, c0, c1, w0, w1, *refs
):
    dq_ref, g0, g1, g2, g3, g4, all_ref = refs[given:]
    head = pl.program_id(0)

    @pl.when(head == 0)
    def _():
        total = near_ref[...] + dot(c0[...], w0[...], NN) + dot(c1[...], w1[...], NN)
        all_ref[...] = total.astype(BF)

    grads = (g0, g1, g2, g3, g4)
    q = q_ref[...]
    do = all_ref[:, pl.ds(pl.multiple_of(head * HEAD, HEAD), HEAD)]
    rows = k0.shape[0]
    do_t = do.T
    delta = jnp.sum(
        do_t.astype(F32) * att_ref[...].T.astype(F32), axis=0, keepdims=True
    )
    score_grads = []
    for i, v in enumerate((v0, v1, v2, v3, v4)):
        p = p_ref[0, rows * i : rows * (i + 1), :]
        prob_grad = dot(v[...], do_t, NN)
        ds = (p.astype(F32) * (prob_grad - delta)).astype(BF)
        score_grads.append(ds)
        grads[i][0] = (dot(ds, q, NN) * SCALE).astype(grads[i].dtype)
        grads[i][1] = dot(p, do, NN).astype(grads[i].dtype)
    keys = jnp.concatenate([k[...] for k in (k0, k1, k2, k3, k4)], axis=0)
    dq_ref[...] = (dot(keys, jnp.concatenate(score_grads, axis=0), TN) * SCALE).T


def call(kernel, grid, scalars, in_specs, out_specs, out_shape, scratch=(), name=None, cost=None):
    return pl.pallas_call(
        kernel,
        grid_spec=pltpu.PrefetchScalarGridSpec(
            num_scalar_prefetch=len(scalars),
            grid=grid,
            in_specs=in_specs,
            out_specs=out_specs,
            scratch_shapes=scratch,
        ),
        out_shape=out_shape,
        compiler_params=pltpu.CompilerParams(vmem_limit_bytes=VMEM),
        cost_estimate=cost,
        name=name,
    )


def whole(v):
    return pl.BlockSpec(v.shape, lambda *_: (0,) * len(v.shape))


def weight_far_kernel(pos, l0, l1, att_ref, gw_ref, far0, far1):
    weight_rows((l0, l1), att_ref, gw_ref)
    far0[...] = gw_ref[0, pos[FAR]]
    far1[...] = gw_ref[1, pos[FAR]]


def weight_far(pos, l0, l1, att):
    part, feature = l0.shape[1] // RING, att.shape[1]
    far = jax.ShapeDtypeStruct((part, feature), BF)
    shapes = [jax.ShapeDtypeStruct((2, RING, part, feature), BF), far, far]
    return call(
        weight_far_kernel,
        (1,),
        (pos,),
        [whole(l0), whole(l1), whole(att)],
        [whole(v) for v in shapes],
        shapes,
        name="weight_far",
    )(pos, l0, l1, att)


def beside_kernel(pos, even, odd, got_even, got_odd, to_even, to_odd):
    to_even[0] = even[0, 0]
    to_even[1] = (even[1, 0].astype(F32) + got_odd[...].astype(F32)).astype(BF)
    to_odd[0] = (odd[0, 0].astype(F32) + got_even[...].astype(F32)).astype(BF)
    to_odd[1] = odd[1, 0]


def beside(pos, chunks, got):
    _, _, part, feature = chunks.shape
    send = jax.ShapeDtypeStruct((2, part, feature), BF)
    pick = lambda k: pl.BlockSpec((2, 1, part, feature), lambda i, pos: (0, pos[k], 0, 0))
    return call(
        beside_kernel,
        (1,),
        (pos,),
        [pick(EVEN), pick(ODD), whole(got[0]), whole(got[1])],
        [whole(send)] * 2,
        [send] * 2,
        name="beside",
    )(pos, chunks, chunks, *got)


def rows_kernel(pos, near, near_even, near_odd, more, more_even, more_odd, keep, s1, s2, s3, rows):
    for j, (own, even, odd) in enumerate(((near, near_even, near_odd), (more, more_even, more_odd))):
        total = own[:, 0].astype(F32) + even[...].astype(F32) + odd[...].astype(F32)
        rows[2 * j : 2 * j + 2] = total.astype(BF)
    for k, out in enumerate((keep, s1, s2, s3)):
        out[...] = rows[pos[PART + k]]


def rows_of(pos, near, near_got, more, more_got):
    _, _, part, feature = near.shape
    send = jax.ShapeDtypeStruct((part, feature), BF)
    own = pl.BlockSpec((2, 1, part, feature), lambda i, pos: (0, pos[OWN], 0, 0))
    got = whole(near_got[0])
    return call(
        rows_kernel,
        (1,),
        (pos,),
        [own, got, got] * 2,
        [whole(send)] * 4,
        [send] * 4,
        scratch=[pltpu.VMEM((RING, part, feature), BF)],
        name="rows",
    )(pos, near, *near_got, more, *more_got)


def plane_kernel(pos, own, g1, g2, g3, keep, s1, s2, s3, rows):
    each = own.shape[0] // RING
    total = own[...].astype(F32) + g1[...].astype(F32) + g2[...].astype(F32) + g3[...].astype(F32)
    for i in range(RING):
        rows[i] = total[i * each : (i + 1) * each]
    keep[...] = rows[pos[SHARE]]
    for k, out in enumerate((s1, s2, s3)):
        out[...] = rows[pos[SHARE + 1 + k]].astype(BF)


def plane_of(pos, own, got):
    part, feature = own.shape
    each = part // RING
    shapes = [jax.ShapeDtypeStruct((each, feature), F32)] + [jax.ShapeDtypeStruct((each, feature), BF)] * 3
    return call(
        plane_kernel,
        (1,),
        (pos,),
        [whole(own)] + [whole(v) for v in got],
        [whole(v) for v in shapes],
        shapes,
        scratch=[pltpu.VMEM((RING, each, feature), F32)],
        name="plane",
    )(pos, own, *got)


def forward_call(pos, q, keys, values, bias, weight, lefts):
    tokens, feature = q.shape
    heads = feature // HEAD
    rows = keys[0].shape[0]
    band = rows * len(keys)
    part = feature // RING
    by_head = pl.BlockSpec((tokens, HEAD), lambda h, pos: (0, h))
    kv_head = pl.BlockSpec((rows, HEAD), lambda h, pos: (0, h))
    once = [
        jax.ShapeDtypeStruct((tokens, weight.shape[0]), BF),
        jax.ShapeDtypeStruct((2, RING, part, feature), BF),
        jax.ShapeDtypeStruct((part, feature), BF),
        jax.ShapeDtypeStruct((part, feature), BF),
    ]
    return call(
        attend_forward,
        (heads,),
        (pos,),
        [by_head] + [kv_head] * 10 + [whole(v) for v in (bias, weight, *lefts)],
        [by_head, pl.BlockSpec((1, band, tokens), lambda h, pos: (h, 0, 0))] + [whole(v) for v in once],
        [
            jax.ShapeDtypeStruct((tokens, feature), BF),
            jax.ShapeDtypeStruct((heads, band, tokens), BF),
        ]
        + once,
        scratch=[pltpu.VMEM((tokens, feature), BF)],
        name="attend_forward",
        cost=pl.CostEstimate(
            flops=8 * tokens * band * feature, bytes_accessed=0, transcendentals=heads * band * tokens
        ),
    )(pos, q, *keys, *values, bias, weight, *lefts)


def backward_call(q, keys, values, p, att, near, cots, weights, half, done):
    tokens, feature = q.shape
    heads = feature // HEAD // 2
    first = half * heads
    rows = keys[0].shape[0]
    band = rows * len(keys)
    by_head = pl.BlockSpec((tokens, HEAD), lambda h: (0, first + h))
    kv_head = pl.BlockSpec((rows, HEAD), lambda h: (0, first + h))
    both_head = pl.BlockSpec((2, rows, HEAD), lambda h: (0, 0, first + h))
    columns = lambda v: pl.BlockSpec((v.shape[0], feature // 2), lambda h: (0, half))
    piece = lambda kind: jax.ShapeDtypeStruct((2, rows, feature), kind)
    given = 18
    return pl.pallas_call(
        functools.partial(attend_backward, len(done)),
        grid=(heads,),
        in_specs=[by_head]
        + [kv_head] * 10
        + [pl.BlockSpec((1, band, tokens), lambda h: (first + h, 0, 0)), by_head, columns(near)]
        + [whole(v) for v in cots]
        + [columns(v) for v in weights]
        + [pl.BlockSpec(memory_space=pl.ANY)] * len(done),
        out_specs=[by_head] + [both_head] * 5,
        out_shape=[jax.ShapeDtypeStruct((tokens, feature), F32)]
        + [piece(F32), piece(F32), piece(F32), piece(BF), piece(BF)],
        scratch_shapes=[pltpu.VMEM((tokens, feature // 2), BF)],
        input_output_aliases={given + i: i for i in range(len(done))},
        compiler_params=pltpu.CompilerParams(vmem_limit_bytes=VMEM),
        cost_estimate=pl.CostEstimate(
            flops=6 * tokens * band * feature, bytes_accessed=0, transcendentals=0
        ),
        name="attend_backward",
    )(q, *keys, *values, p, att, near, *cots, *weights, *done)


def place(s):
    return s // (RING * RING), (s // RING) % RING, s % RING


def index(y, x, z):
    return (y * RING + x) * RING + z


FAR, EVEN, ODD, OWN, PART, SHARE, WEIGHT, AUDIO = 0, 1, 2, 3, 4, 8, 12, 16


def table(shards, per_shard):
    rows = []
    for s in range(shards):
        y, x, z = place(s)
        step = 1 - 2 * (s % 2)
        for a in range(4):
            row = [(x + 2) % RING, x ^ 1, odd_swap(x, RING), x]
            row += [y ^ j ^ a for j in range(RING)] + [z ^ j for j in range(RING)]
            row += [a ^ j for j in range(4)]
            for shard in (s, s + step, s - step, s + 2 * step, s - 2 * step):
                row += [shard * per_shard + i for i in range(per_shard)]
            rows.append(row)
    return np.array(rows, np.int32)


def odd_swap(i, n):
    return (((i + 1) % n ^ 1) - 1) % n


def pick(array, i):
    return lax.dynamic_index_in_dim(array, i, 0, keepdims=False, allow_negative_indices=False)


def after(value, *earlier):
    return lax.optimization_barrier((value, *earlier))[0]


def add_half(own, got):
    return (own.astype(F32) + got.astype(F32)).astype(BF)


def local(video_query, audio_key, audio_value, window_first, window_count, out_weight, cotangent):
    tokens, feature = video_query.shape
    audio_rows = audio_key.shape[0]
    shards = lax.axis_size("vseq")
    device = lax.axis_index("vseq") * 4 + lax.axis_index("aseq")
    pos = pick(jnp.asarray(table(shards, audio_rows // ABLK)), device)
    each = range(shards)
    pa = [(i, i ^ 1) for i in each]
    pb = [(i, odd_swap(i, shards)) for i in each]

    def along(change):
        return [(i, index(*change(*place(i)))) for i in each]

    x_even = along(lambda y, x, z: (y, x ^ 1, z))
    x_odd = along(lambda y, x, z: (y, odd_swap(x, RING), z))

    def exchange(send, even, odd):
        return lax.ppermute(send[0], "vseq", even), lax.ppermute(send[1], "vseq", odd)

    def direct(sends, change):
        return [
            lax.ppermute(send, "vseq", along(functools.partial(change, j + 1)))
            for j, send in enumerate(sends)
        ]

    key_block = pos[AUDIO:]
    first = jnp.repeat(window_first, VBLK)
    end = jnp.repeat(window_first + window_count, VBLK)
    allowed = (key_block[:, None] >= first[None, :]) & (key_block[:, None] < end[None, :])
    bias = jnp.where(allowed, 0.0, -1e30).astype(F32)

    weight_parts = out_weight.reshape(4, feature, feature)
    w0, w1, w2, w3 = [
        pick(weight_parts, pos[WEIGHT + j]) for j in range(4)
    ]
    w_core = jnp.concatenate([w3, w1], 0)
    cot_core = lax.ppermute(cotangent, "aseq", CORE)
    grad_near = dot(cot_core, w1, NN) + dot(cotangent, w0, NN)

    def halo(own, *first):
        by_a = lax.ppermute(own, "vseq", pa)
        by_b = lax.ppermute(own, "vseq", pb)
        by_a, by_b = after((by_a, by_b), *first)
        return own, by_a, by_b, lax.ppermute(by_b, "vseq", pa), lax.ppermute(by_a, "vseq", pb)

    keys = halo(after(audio_key, pos), bias)
    values = halo(audio_value, grad_near, w_core)

    cot_pair = lax.ppermute(after(cotangent, *keys[3:], *values[3:]), "aseq", PAIR)
    att, p, far_core, near, *near_far = forward_call(
        pos, video_query, keys, values, after(bias, grad_near, w2, w3), w_core, (cotangent, cot_core)
    )

    near_got = exchange(near_far, x_even, x_odd)
    cot_pair = after(cot_pair, *near_got)
    cot_both = lax.ppermute(cot_pair, "aseq", CORE)
    got_core = lax.ppermute(after(far_core, cot_pair), "aseq", CORE)
    near_send = beside(pos, near, near_got)
    near_got = exchange(near_send, x_even, x_odd)
    far_pair = (dot(after(att, *near_send), w2, NT) + got_core[:, :feature].astype(F32)).astype(BF)
    got_pair = lax.ppermute(far_pair, "aseq", PAIR)
    more, *more_far = weight_far(pos, cot_pair, after(cot_both, far_pair), att)
    more_got = exchange(more_far, x_even, x_odd)

    def backward(half, cot_both, done):
        return backward_call(
            video_query, keys, values, p, att, grad_near, (cot_pair, cot_both), (w2, w3), half, done
        )

    left = backward(0, after(cot_both, *more_far), ())
    more_send = beside(pos, more, after(more_got, left[0], *near_got))
    more_got = exchange(more_send, x_even, x_odd)
    mixed_video = (
        dot(after(att, *more_send), w0, NT) + got_core[:, feature:].astype(F32) + got_pair.astype(F32)
    ).astype(BF)
    grad_query, g_own, g_a, g_b, g_aa, g_bb = backward(1, after(cot_both, mixed_video), left)
    back_a = lax.ppermute(g_aa, "vseq", pa)
    back_b = lax.ppermute(g_bb, "vseq", pb)

    keep, *sends = rows_of(pos, near, near_got, more, more_got)
    y_got = direct(sends, lambda j, y, x, z: (y ^ j, x, z))

    back_a, back_b = after((back_a, back_b), keep)
    send_b = add_half(g_b, back_a)
    send_a = add_half(g_a, back_b)
    sum_b = lax.ppermute(send_b, "vseq", pb)
    sum_a = lax.ppermute(send_a, "vseq", pa)

    grad_weight, *sends = plane_of(pos, after(keep, send_a, send_b), y_got)
    for got in direct(sends, lambda j, y, x, z: (y, x, z ^ j)):
        grad_weight = grad_weight + got.astype(F32)

    grad_key = g_own[0] + sum_a[0].astype(F32) + sum_b[0].astype(F32)
    grad_value = g_own[1] + sum_a[1].astype(F32) + sum_b[1].astype(F32)
    return mixed_video, grad_query, grad_key, grad_value, grad_weight


def solution(mesh):
    both = P("vseq", "aseq")
    in_specs = (both, both, both, P("vseq"), P("vseq"), P(None, "aseq"), both)
    return jax.shard_map(
        local, mesh=mesh, in_specs=in_specs, out_specs=(both,) * 5, check_vma=False
    )
```

```python
import functools
import math

import jax
import jax.numpy as jnp
import numpy as np
from jax import lax
from jax.experimental import pallas as pl
from jax.experimental.pallas import tpu as pltpu
from jax.sharding import PartitionSpec as P

HEAD = 128
VBLK = 128
ABLK = 32
RING = 4
PAIRED = 2
SCALE = 1.0 / math.sqrt(HEAD)
LOG2E = math.log2(math.e)
NT = (((1,), (1,)), ((), ()))
TN = (((0,), (0,)), ((), ()))
NN = (((1,), (0,)), ((), ()))
F32 = jnp.float32
BF = jnp.bfloat16
VMEM = 24 << 20
CORE = [(a, a ^ 1) for a in range(4)]
PAIR = [(a, a ^ 2) for a in range(4)]


def dot(a, b, dims):
    return lax.dot_general(a, b, dims, preferred_element_type=F32)


def attend_forward(
    pos, q_ref, k0, k1, k2, k3, k4, v0, v1, v2, v3, v4, bias_ref, w_ref, l0, l1,
    att_ref, p_ref, out_ref, gw_ref, far0, far1, all_ref,
):
    tokens = q_ref.shape[0]
    rows = k0.shape[0]
    blocks = rows // ABLK
    head = pl.program_id(0)
    for u in range(PAIRED):
        own = slice(u * HEAD, (u + 1) * HEAD)
        q = q_ref[:, own]
        scores = []
        for i, k in enumerate((k0, k1, k2, k3, k4)):
            tile = dot(k[:, own], q, NT).reshape(blocks, ABLK, tokens)
            tile = tile + bias_ref[blocks * i : blocks * (i + 1), :][:, None, :]
            scores.append(tile.reshape(rows, tokens))
        top = jnp.max(functools.reduce(jnp.maximum, scores), axis=0, keepdims=True)
        exponent = [jnp.exp2((tile - top) * (SCALE * LOG2E)) for tile in scores]
        total = jnp.sum(functools.reduce(jnp.add, exponent), axis=0, keepdims=True)
        share = 1.0 / total
        for i, tile in enumerate(exponent):
            p_ref[u, rows * i : rows * (i + 1), :] = (tile * share).astype(BF)
        values = jnp.concatenate([v[:, own] for v in (v0, v1, v2, v3, v4)], axis=0)
        att_ref[:, own] = dot(values, p_ref[u], TN).T.astype(BF)
    all_ref[:, pl.ds(pl.multiple_of(head * PAIRED * HEAD, PAIRED * HEAD), PAIRED * HEAD)] = att_ref[...]

    @pl.when(head == pl.num_programs(0) - 1)
    def _():
        out_ref[...] = dot(all_ref[...], w_ref[...], NT).astype(BF)
        weight_rows((l0, l1), all_ref, gw_ref)
        far0[...] = gw_ref[0, pos[FAR]]
        far1[...] = gw_ref[1, pos[FAR]]


def weight_rows(lefts, att_ref, gw_ref):
    part = gw_ref.shape[2]
    for j, left in enumerate(lefts):
        rows = dot(left[...], att_ref[...], TN).astype(BF)
        for i in range(RING):
            gw_ref[j, i] = rows[i * part : (i + 1) * part]


def attend_backward(
    q_ref, k0, k1, k2, k3, k4, v0, v1, v2, v3, v4, p_ref, att_ref, near_ref, c0, c1, w0, w1,
    dq_ref, g0, g1, g2, g3, g4, all_ref,
):
    head = pl.program_id(0)

    @pl.when(head == 0)
    def _():
        total = near_ref[...] + dot(c0[...], w0[...], NN) + dot(c1[...], w1[...], NN)
        all_ref[...] = total.astype(BF)

    grads = (g0, g1, g2, g3, g4)
    rows = k0.shape[0]
    wide = all_ref[:, pl.ds(pl.multiple_of(head * PAIRED * HEAD, PAIRED * HEAD), PAIRED * HEAD)]
    for u in range(PAIRED):
        own = slice(u * HEAD, (u + 1) * HEAD)
        q = q_ref[:, own]
        do = wide[:, own]
        do_t = do.T
        delta = jnp.sum(
            do_t.astype(F32) * att_ref[:, own].T.astype(F32), axis=0, keepdims=True
        )
        values = jnp.concatenate([v[:, own] for v in (v0, v1, v2, v3, v4)], axis=0)
        keys = jnp.concatenate([k[:, own] for k in (k0, k1, k2, k3, k4)], axis=0)
        p = p_ref[u]
        ds = (p.astype(F32) * (dot(values, do_t, NN) - delta)).astype(BF)
        dk = dot(ds, q, NN) * SCALE
        dv = dot(p, do, NN)
        for i, out in enumerate((g0, g1, g2, g3, g4)):
            out[0, :, own] = dk[rows * i : rows * (i + 1)].astype(out.dtype)
            out[1, :, own] = dv[rows * i : rows * (i + 1)].astype(out.dtype)
        dq_ref[:, own] = (dot(keys, ds, TN) * SCALE).T


def call(kernel, grid, scalars, in_specs, out_specs, out_shape, scratch=(), name=None, cost=None):
    return pl.pallas_call(
        kernel,
        grid_spec=pltpu.PrefetchScalarGridSpec(
            num_scalar_prefetch=len(scalars),
            grid=grid,
            in_specs=in_specs,
            out_specs=out_specs,
            scratch_shapes=scratch,
        ),
        out_shape=out_shape,
        compiler_params=pltpu.CompilerParams(vmem_limit_bytes=VMEM),
        cost_estimate=cost,
        name=name,
    )


def whole(v):
    return pl.BlockSpec(v.shape, lambda *_: (0,) * len(v.shape))


def weight_far_kernel(pos, l0, l1, att_ref, gw_ref, far0, far1):
    weight_rows((l0, l1), att_ref, gw_ref)
    far0[...] = gw_ref[0, pos[FAR]]
    far1[...] = gw_ref[1, pos[FAR]]


def weight_far(pos, l0, l1, att):
    part, feature = l0.shape[1] // RING, att.shape[1]
    far = jax.ShapeDtypeStruct((part, feature), BF)
    shapes = [jax.ShapeDtypeStruct((2, RING, part, feature), BF), far, far]
    return call(
        weight_far_kernel,
        (1,),
        (pos,),
        [whole(l0), whole(l1), whole(att)],
        [whole(v) for v in shapes],
        shapes,
        name="weight_far",
    )(pos, l0, l1, att)


def beside_kernel(pos, even, odd, got_even, got_odd, to_even, to_odd):
    to_even[0] = even[0, 0]
    to_even[1] = (even[1, 0].astype(F32) + got_odd[...].astype(F32)).astype(BF)
    to_odd[0] = (odd[0, 0].astype(F32) + got_even[...].astype(F32)).astype(BF)
    to_odd[1] = odd[1, 0]


def beside(pos, chunks, got):
    _, _, part, feature = chunks.shape
    send = jax.ShapeDtypeStruct((2, part, feature), BF)
    pick = lambda k: pl.BlockSpec((2, 1, part, feature), lambda i, pos: (0, pos[k], 0, 0))
    return call(
        beside_kernel,
        (1,),
        (pos,),
        [pick(EVEN), pick(ODD), whole(got[0]), whole(got[1])],
        [whole(send)] * 2,
        [send] * 2,
        name="beside",
    )(pos, chunks, chunks, *got)


def rows_kernel(pos, near, near_even, near_odd, more, more_even, more_odd, keep, s1, s2, s3, rows):
    for j, (own, even, odd) in enumerate(((near, near_even, near_odd), (more, more_even, more_odd))):
        total = own[:, 0].astype(F32) + even[...].astype(F32) + odd[...].astype(F32)
        rows[2 * j : 2 * j + 2] = total.astype(BF)
    for k, out in enumerate((keep, s1, s2, s3)):
        out[...] = rows[pos[PART + k]]


def rows_of(pos, near, near_got, more, more_got):
    _, _, part, feature = near.shape
    send = jax.ShapeDtypeStruct((part, feature), BF)
    own = pl.BlockSpec((2, 1, part, feature), lambda i, pos: (0, pos[OWN], 0, 0))
    got = whole(near_got[0])
    return call(
        rows_kernel,
        (1,),
        (pos,),
        [own, got, got] * 2,
        [whole(send)] * 4,
        [send] * 4,
        scratch=[pltpu.VMEM((RING, part, feature), BF)],
        name="rows",
    )(pos, near, *near_got, more, *more_got)


def plane_kernel(pos, own, g1, g2, g3, keep, s1, s2, s3, rows):
    each = own.shape[0] // RING
    total = own[...].astype(F32) + g1[...].astype(F32) + g2[...].astype(F32) + g3[...].astype(F32)
    for i in range(RING):
        rows[i] = total[i * each : (i + 1) * each]
    keep[...] = rows[pos[SHARE]]
    for k, out in enumerate((s1, s2, s3)):
        out[...] = rows[pos[SHARE + 1 + k]].astype(BF)


def plane_of(pos, own, got):
    part, feature = own.shape
    each = part // RING
    shapes = [jax.ShapeDtypeStruct((each, feature), F32)] + [jax.ShapeDtypeStruct((each, feature), BF)] * 3
    return call(
        plane_kernel,
        (1,),
        (pos,),
        [whole(own)] + [whole(v) for v in got],
        [whole(v) for v in shapes],
        shapes,
        scratch=[pltpu.VMEM((RING, each, feature), F32)],
        name="plane",
    )(pos, own, *got)


def forward_call(pos, q, keys, values, bias, weight, lefts):
    tokens, feature = q.shape
    heads = feature // HEAD
    rows = keys[0].shape[0]
    band = rows * len(keys)
    part = feature // RING
    by_head = pl.BlockSpec((tokens, PAIRED * HEAD), lambda h, pos: (0, h))
    kv_head = pl.BlockSpec((rows, PAIRED * HEAD), lambda h, pos: (0, h))
    once = [
        jax.ShapeDtypeStruct((tokens, weight.shape[0]), BF),
        jax.ShapeDtypeStruct((2, RING, part, feature), BF),
        jax.ShapeDtypeStruct((part, feature), BF),
        jax.ShapeDtypeStruct((part, feature), BF),
    ]
    return call(
        attend_forward,
        (heads // PAIRED,),
        (pos,),
        [by_head] + [kv_head] * 10 + [whole(v) for v in (bias, weight, *lefts)],
        [by_head, pl.BlockSpec((PAIRED, band, tokens), lambda h, pos: (h, 0, 0))] + [whole(v) for v in once],
        [
            jax.ShapeDtypeStruct((tokens, feature), BF),
            jax.ShapeDtypeStruct((heads, band, tokens), BF),
        ]
        + once,
        scratch=[pltpu.VMEM((tokens, feature), BF)],
        name="attend_forward",
        cost=pl.CostEstimate(
            flops=8 * tokens * band * feature, bytes_accessed=0, transcendentals=heads * band * tokens
        ),
    )(pos, q, *keys, *values, bias, weight, *lefts)


def backward_call(q, keys, values, p, att, near, cots, weights):
    tokens, feature = q.shape
    heads = feature // HEAD
    rows = keys[0].shape[0]
    band = rows * len(keys)
    by_head = pl.BlockSpec((tokens, PAIRED * HEAD), lambda h: (0, h))
    kv_head = pl.BlockSpec((rows, PAIRED * HEAD), lambda h: (0, h))
    both_head = pl.BlockSpec((2, rows, PAIRED * HEAD), lambda h: (0, 0, h))
    piece = lambda kind: jax.ShapeDtypeStruct((2, rows, feature), kind)
    return call(
        attend_backward,
        (heads // PAIRED,),
        (),
        [by_head]
        + [kv_head] * 10
        + [pl.BlockSpec((PAIRED, band, tokens), lambda h: (h, 0, 0)), by_head]
        + [whole(v) for v in (near, *cots, *weights)],
        [by_head] + [both_head] * 5,
        [jax.ShapeDtypeStruct((tokens, feature), F32)]
        + [piece(F32), piece(F32), piece(F32), piece(BF), piece(BF)],
        scratch=[pltpu.VMEM((tokens, feature), BF)],
        name="attend_backward",
        cost=pl.CostEstimate(
            flops=12 * tokens * band * feature, bytes_accessed=0, transcendentals=0
        ),
    )(q, *keys, *values, p, att, near, *cots, *weights)


def place(s):
    return s // (RING * RING), (s // RING) % RING, s % RING


def index(y, x, z):
    return (y * RING + x) * RING + z


FAR, EVEN, ODD, OWN, PART, SHARE, WEIGHT, AUDIO = 0, 1, 2, 3, 4, 8, 12, 16


def table(shards, per_shard):
    rows = []
    for s in range(shards):
        y, x, z = place(s)
        step = 1 - 2 * (s % 2)
        for a in range(4):
            row = [(x + 2) % RING, x ^ 1, odd_swap(x, RING), x]
            row += [y ^ j ^ a for j in range(RING)] + [z ^ j for j in range(RING)]
            row += [a ^ j for j in range(4)]
            for shard in (s, s + step, s - step, s + 2 * step, s - 2 * step):
                row += [shard * per_shard + i for i in range(per_shard)]
            rows.append(row)
    return np.array(rows, np.int32)


def odd_swap(i, n):
    return (((i + 1) % n ^ 1) - 1) % n


def pick(array, i):
    return lax.dynamic_index_in_dim(array, i, 0, keepdims=False, allow_negative_indices=False)


def after(value, *earlier):
    return lax.optimization_barrier((value, *earlier))[0]


def add_half(own, got):
    return (own.astype(F32) + got.astype(F32)).astype(BF)


def local(video_query, audio_key, audio_value, window_first, window_count, out_weight, cotangent):
    tokens, feature = video_query.shape
    audio_rows = audio_key.shape[0]
    shards = lax.axis_size("vseq")
    device = lax.axis_index("vseq") * 4 + lax.axis_index("aseq")
    pos = pick(jnp.asarray(table(shards, audio_rows // ABLK)), device)
    each = range(shards)
    pa = [(i, i ^ 1) for i in each]
    pb = [(i, odd_swap(i, shards)) for i in each]

    def along(change):
        return [(i, index(*change(*place(i)))) for i in each]

    x_even = along(lambda y, x, z: (y, x ^ 1, z))
    x_odd = along(lambda y, x, z: (y, odd_swap(x, RING), z))

    def exchange(send, even, odd):
        return lax.ppermute(send[0], "vseq", even), lax.ppermute(send[1], "vseq", odd)

    def direct(sends, change):
        return [
            lax.ppermute(send, "vseq", along(functools.partial(change, j + 1)))
            for j, send in enumerate(sends)
        ]

    key_block = pos[AUDIO:]
    first = jnp.repeat(window_first, VBLK)
    end = jnp.repeat(window_first + window_count, VBLK)
    allowed = (key_block[:, None] >= first[None, :]) & (key_block[:, None] < end[None, :])
    bias = jnp.where(allowed, 0.0, -1e30).astype(F32)

    weight_parts = out_weight.reshape(4, feature, feature)
    w0, w1, w2, w3 = [
        pick(weight_parts, pos[WEIGHT + j]) for j in range(4)
    ]
    w_core = jnp.concatenate([w3, w1], 0)
    cot_core = lax.ppermute(cotangent, "aseq", CORE)
    grad_near = dot(cot_core, w1, NN) + dot(cotangent, w0, NN)

    def halo(own, *first):
        by_a = lax.ppermute(own, "vseq", pa)
        by_b = lax.ppermute(own, "vseq", pb)
        by_a, by_b = after((by_a, by_b), *first)
        return own, by_a, by_b, lax.ppermute(by_b, "vseq", pa), lax.ppermute(by_a, "vseq", pb)

    keys = halo(after(audio_key, pos), bias)
    values = halo(audio_value, grad_near, w_core)

    cot_pair = lax.ppermute(after(cotangent, *keys[3:], *values[3:]), "aseq", PAIR)
    att, p, far_core, near, *near_far = forward_call(
        pos, video_query, keys, values, after(bias, grad_near, w2, w3), w_core, (cotangent, cot_core)
    )

    near_got = exchange(near_far, x_even, x_odd)
    cot_pair = after(cot_pair, *near_got)
    cot_both = lax.ppermute(cot_pair, "aseq", CORE)
    got_core = lax.ppermute(after(far_core, cot_pair), "aseq", CORE)
    near_send = beside(pos, near, near_got)
    near_got = exchange(near_send, x_even, x_odd)
    far_pair = (dot(after(att, *near_send), w2, NT) + got_core[:, :feature].astype(F32)).astype(BF)
    got_pair = lax.ppermute(far_pair, "aseq", PAIR)
    more, *more_far = weight_far(pos, cot_pair, after(cot_both, far_pair), att)
    more_got = exchange(more_far, x_even, x_odd)

    grad_query, g_own, g_a, g_b, g_aa, g_bb = backward_call(
        video_query, keys, values, p, att, grad_near, (cot_pair, after(cot_both, *more_far)), (w2, w3)
    )
    back_a = lax.ppermute(g_aa, "vseq", pa)
    back_b = lax.ppermute(g_bb, "vseq", pb)

    more_send = beside(pos, more, after(more_got, g_aa, g_bb, *near_got))
    more_got = exchange(more_send, x_even, x_odd)
    mixed_video = (
        dot(after(att, *more_send), w0, NT) + got_core[:, feature:].astype(F32) + got_pair.astype(F32)
    ).astype(BF)
    keep, *sends = rows_of(pos, near, near_got, more, after(more_got, mixed_video))
    y_got = direct(sends, lambda j, y, x, z: (y ^ j, x, z))

    back_a, back_b = after((back_a, back_b), keep)
    send_b = add_half(g_b, back_a)
    send_a = add_half(g_a, back_b)
    sum_b = lax.ppermute(send_b, "vseq", pb)
    sum_a = lax.ppermute(send_a, "vseq", pa)

    grad_weight, *sends = plane_of(pos, after(keep, send_a, send_b), y_got)
    for got in direct(sends, lambda j, y, x, z: (y, x, z ^ j)):
        grad_weight = grad_weight + got.astype(F32)

    grad_key = g_own[0] + sum_a[0].astype(F32) + sum_b[0].astype(F32)
    grad_value = g_own[1] + sum_a[1].astype(F32) + sum_b[1].astype(F32)
    return mixed_video, grad_query, grad_key, grad_value, grad_weight


def solution(mesh):
    both = P("vseq", "aseq")
    in_specs = (both, both, both, P("vseq"), P("vseq"), P(None, "aseq"), both)
    return jax.shard_map(
        local, mesh=mesh, in_specs=in_specs, out_specs=(both,) * 5, check_vma=False
    )
```

```python
import functools
import math

import jax
import jax.numpy as jnp
import numpy as np
from jax import lax
from jax.experimental import pallas as pl
from jax.experimental.pallas import tpu as pltpu
from jax.sharding import PartitionSpec as P

HEAD = 128
VBLK = 128
ABLK = 32
RING = 4
PAIRED = 2
SCALE = 1.0 / math.sqrt(HEAD)
LOG2E = math.log2(math.e)
NT = (((1,), (1,)), ((), ()))
TN = (((0,), (0,)), ((), ()))
NN = (((1,), (0,)), ((), ()))
F32 = jnp.float32
BF = jnp.bfloat16
VMEM = 24 << 20
CORE = [(a, a ^ 1) for a in range(4)]
PAIR = [(a, a ^ 2) for a in range(4)]


def dot(a, b, dims):
    return lax.dot_general(a, b, dims, preferred_element_type=F32)


def attend_forward(
    pos, q_ref, k0, k1, k2, k3, k4, v0, v1, v2, v3, v4, bias_ref, w_ref, l0, l1,
    att_ref, p_ref, out_ref, gw_ref, far0, far1, all_ref,
):
    tokens = q_ref.shape[0]
    rows = k0.shape[0]
    blocks = rows // ABLK
    head = pl.program_id(0)
    for u in range(PAIRED):
        own = slice(u * HEAD, (u + 1) * HEAD)
        q = q_ref[:, own]
        scores = []
        for i, k in enumerate((k0, k1, k2, k3, k4)):
            tile = dot(k[:, own], q, NT).reshape(blocks, ABLK, tokens)
            tile = tile + bias_ref[blocks * i : blocks * (i + 1), :][:, None, :]
            scores.append(tile.reshape(rows, tokens))
        top = jnp.max(functools.reduce(jnp.maximum, scores), axis=0, keepdims=True)
        exponent = [jnp.exp2((tile - top) * (SCALE * LOG2E)) for tile in scores]
        total = jnp.sum(functools.reduce(jnp.add, exponent), axis=0, keepdims=True)
        share = 1.0 / total
        for i, tile in enumerate(exponent):
            p_ref[u, rows * i : rows * (i + 1), :] = (tile * share).astype(BF)
        values = jnp.concatenate([v[:, own] for v in (v0, v1, v2, v3, v4)], axis=0)
        att_ref[:, own] = dot(values, p_ref[u], TN).T.astype(BF)
    all_ref[:, pl.ds(pl.multiple_of(head * PAIRED * HEAD, PAIRED * HEAD), PAIRED * HEAD)] = att_ref[...]

    @pl.when(head == pl.num_programs(0) - 1)
    def _():
        out_ref[...] = dot(all_ref[...], w_ref[...], NT).astype(BF)
        weight_rows((l0, l1), all_ref, gw_ref)
        far0[...] = gw_ref[0, pos[FAR]]
        far1[...] = gw_ref[1, pos[FAR]]


def weight_rows(lefts, att_ref, gw_ref):
    part = gw_ref.shape[2]
    for j, left in enumerate(lefts):
        rows = dot(left[...], att_ref[...], TN).astype(BF)
        for i in range(RING):
            gw_ref[j, i] = rows[i * part : (i + 1) * part]


def attend_backward(
    q_ref, k0, k1, k2, k3, k4, v0, v1, v2, v3, v4, p_ref, att_ref, near_ref, c0, c1, w0, w1,
    dq_ref, g0, g1, g2, g3, g4, all_ref,
):
    head = pl.program_id(0)

    @pl.when(head == 0)
    def _():
        total = near_ref[...] + dot(c0[...], w0[...], NN) + dot(c1[...], w1[...], NN)
        all_ref[...] = total.astype(BF)

    grads = (g0, g1, g2, g3, g4)
    rows = k0.shape[0]
    wide = all_ref[:, pl.ds(pl.multiple_of(head * PAIRED * HEAD, PAIRED * HEAD), PAIRED * HEAD)]
    for u in range(PAIRED):
        own = slice(u * HEAD, (u + 1) * HEAD)
        q = q_ref[:, own]
        do = wide[:, own]
        do_t = do.T
        delta = jnp.sum(
            do_t.astype(F32) * att_ref[:, own].T.astype(F32), axis=0, keepdims=True
        )
        values = jnp.concatenate([v[:, own] for v in (v0, v1, v2, v3, v4)], axis=0)
        keys = jnp.concatenate([k[:, own] for k in (k0, k1, k2, k3, k4)], axis=0)
        p = p_ref[u]
        ds = (p.astype(F32) * (dot(values, do_t, NN) - delta)).astype(BF)
        dk = dot(ds, q, NN) * SCALE
        dv = dot(p, do, NN)
        for i, out in enumerate((g0, g1, g2, g3, g4)):
            out[0, :, own] = dk[rows * i : rows * (i + 1)].astype(out.dtype)
            out[1, :, own] = dv[rows * i : rows * (i + 1)].astype(out.dtype)
        dq_ref[:, own] = (dot(keys, ds, TN) * SCALE).T


def call(kernel, grid, scalars, in_specs, out_specs, out_shape, scratch=(), name=None, cost=None):
    return pl.pallas_call(
        kernel,
        grid_spec=pltpu.PrefetchScalarGridSpec(
            num_scalar_prefetch=len(scalars),
            grid=grid,
            in_specs=in_specs,
            out_specs=out_specs,
            scratch_shapes=scratch,
        ),
        out_shape=out_shape,
        compiler_params=pltpu.CompilerParams(vmem_limit_bytes=VMEM),
        cost_estimate=cost,
        name=name,
    )


def whole(v):
    return pl.BlockSpec(v.shape, lambda *_: (0,) * len(v.shape))


def weight_far_kernel(pos, l0, l1, att_ref, gw_ref, far0, far1):
    weight_rows((l0, l1), att_ref, gw_ref)
    far0[...] = gw_ref[0, pos[FAR]]
    far1[...] = gw_ref[1, pos[FAR]]


def weight_far(pos, l0, l1, att):
    part, feature = l0.shape[1] // RING, att.shape[1]
    far = jax.ShapeDtypeStruct((part, feature), BF)
    shapes = [jax.ShapeDtypeStruct((2, RING, part, feature), BF), far, far]
    return call(
        weight_far_kernel,
        (1,),
        (pos,),
        [whole(l0), whole(l1), whole(att)],
        [whole(v) for v in shapes],
        shapes,
        name="weight_far",
    )(pos, l0, l1, att)


def beside_kernel(pos, even, odd, got_even, got_odd, to_even, to_odd):
    to_even[0] = even[0, 0]
    to_even[1] = (even[1, 0].astype(F32) + got_odd[...].astype(F32)).astype(BF)
    to_odd[0] = (odd[0, 0].astype(F32) + got_even[...].astype(F32)).astype(BF)
    to_odd[1] = odd[1, 0]


def beside(pos, chunks, got):
    _, _, part, feature = chunks.shape
    send = jax.ShapeDtypeStruct((2, part, feature), BF)
    pick = lambda k: pl.BlockSpec((2, 1, part, feature), lambda i, pos: (0, pos[k], 0, 0))
    return call(
        beside_kernel,
        (1,),
        (pos,),
        [pick(EVEN), pick(ODD), whole(got[0]), whole(got[1])],
        [whole(send)] * 2,
        [send] * 2,
        name="beside",
    )(pos, chunks, chunks, *got)


def rows_kernel(pos, near, near_even, near_odd, more, more_even, more_odd, rows, s_even, s_odd):
    for j, (own, even, odd) in enumerate(((near, near_even, near_odd), (more, more_even, more_odd))):
        total = own[:, 0].astype(F32) + even[...].astype(F32) + odd[...].astype(F32)
        rows[2 * j : 2 * j + 2] = total.astype(BF)
    half = s_even.shape[0]
    s_even[...] = rows[pos[PART + 2], :half]
    s_odd[...] = rows[pos[PART + 2], half:]


def rows_of(pos, near, near_got, more, more_got):
    _, _, part, feature = near.shape
    half = jax.ShapeDtypeStruct((part // 2, feature), BF)
    shapes = [jax.ShapeDtypeStruct((RING, part, feature), BF), half, half]
    own = pl.BlockSpec((2, 1, part, feature), lambda i, pos: (0, pos[OWN], 0, 0))
    got = whole(near_got[0])
    return call(
        rows_kernel,
        (1,),
        (pos,),
        [own, got, got] * 2,
        [whole(v) for v in shapes],
        shapes,
        name="rows",
    )(pos, near, *near_got, more, *more_got)


def pass_kernel(pos, rows, got_even, got_odd, to_even, to_odd):
    half = got_even.shape[0]
    to_even[:half] = rows[pos[PART + 1], :half]
    to_even[half:] = (rows[pos[PART + 1], half:].astype(F32) + got_odd[...].astype(F32)).astype(BF)
    to_odd[:half] = (rows[pos[PART + 3], :half].astype(F32) + got_even[...].astype(F32)).astype(BF)
    to_odd[half:] = rows[pos[PART + 3], half:]


def pass_on(pos, rows, got):
    send = jax.ShapeDtypeStruct(rows.shape[1:], BF)
    return call(
        pass_kernel,
        (1,),
        (pos,),
        [whole(v) for v in (rows, *got)],
        [whole(send)] * 2,
        [send] * 2,
        name="pass_on",
    )(pos, rows, *got)


def plane_kernel(pos, own, g1, g2, keep, s1, s2, s3, rows):
    each = own.shape[1] // RING
    total = own[pos[PART]].astype(F32) + g1[...].astype(F32) + g2[...].astype(F32)
    for i in range(RING):
        rows[i] = total[i * each : (i + 1) * each]
    keep[...] = rows[pos[SHARE]]
    for k, out in enumerate((s1, s2, s3)):
        out[...] = rows[pos[SHARE + 1 + k]].astype(BF)


def plane_of(pos, own, got):
    _, part, feature = own.shape
    each = part // RING
    shapes = [jax.ShapeDtypeStruct((each, feature), F32)] + [jax.ShapeDtypeStruct((each, feature), BF)] * 3
    return call(
        plane_kernel,
        (1,),
        (pos,),
        [whole(own)] + [whole(v) for v in got],
        [whole(v) for v in shapes],
        shapes,
        scratch=[pltpu.VMEM((RING, each, feature), F32)],
        name="plane",
    )(pos, own, *got)


def forward_call(pos, q, keys, values, bias, weight, lefts):
    tokens, feature = q.shape
    heads = feature // HEAD
    rows = keys[0].shape[0]
    band = rows * len(keys)
    part = feature // RING
    by_head = pl.BlockSpec((tokens, PAIRED * HEAD), lambda h, pos: (0, h))
    kv_head = pl.BlockSpec((rows, PAIRED * HEAD), lambda h, pos: (0, h))
    once = [
        jax.ShapeDtypeStruct((tokens, weight.shape[0]), BF),
        jax.ShapeDtypeStruct((2, RING, part, feature), BF),
        jax.ShapeDtypeStruct((part, feature), BF),
        jax.ShapeDtypeStruct((part, feature), BF),
    ]
    return call(
        attend_forward,
        (heads // PAIRED,),
        (pos,),
        [by_head] + [kv_head] * 10 + [whole(v) for v in (bias, weight, *lefts)],
        [by_head, pl.BlockSpec((PAIRED, band, tokens), lambda h, pos: (h, 0, 0))] + [whole(v) for v in once],
        [
            jax.ShapeDtypeStruct((tokens, feature), BF),
            jax.ShapeDtypeStruct((heads, band, tokens), BF),
        ]
        + once,
        scratch=[pltpu.VMEM((tokens, feature), BF)],
        name="attend_forward",
        cost=pl.CostEstimate(
            flops=8 * tokens * band * feature, bytes_accessed=0, transcendentals=heads * band * tokens
        ),
    )(pos, q, *keys, *values, bias, weight, *lefts)


def backward_call(q, keys, values, p, att, near, cots, weights):
    tokens, feature = q.shape
    heads = feature // HEAD
    rows = keys[0].shape[0]
    band = rows * len(keys)
    by_head = pl.BlockSpec((tokens, PAIRED * HEAD), lambda h: (0, h))
    kv_head = pl.BlockSpec((rows, PAIRED * HEAD), lambda h: (0, h))
    both_head = pl.BlockSpec((2, rows, PAIRED * HEAD), lambda h: (0, 0, h))
    piece = lambda kind: jax.ShapeDtypeStruct((2, rows, feature), kind)
    return call(
        attend_backward,
        (heads // PAIRED,),
        (),
        [by_head]
        + [kv_head] * 10
        + [pl.BlockSpec((PAIRED, band, tokens), lambda h: (h, 0, 0)), by_head]
        + [whole(v) for v in (near, *cots, *weights)],
        [by_head] + [both_head] * 5,
        [jax.ShapeDtypeStruct((tokens, feature), F32)]
        + [piece(F32), piece(F32), piece(F32), piece(BF), piece(BF)],
        scratch=[pltpu.VMEM((tokens, feature), BF)],
        name="attend_backward",
        cost=pl.CostEstimate(
            flops=12 * tokens * band * feature, bytes_accessed=0, transcendentals=0
        ),
    )(q, *keys, *values, p, att, near, *cots, *weights)


def place(s):
    return s // (RING * RING), (s // RING) % RING, s % RING


def index(y, x, z):
    return (y * RING + x) * RING + z


FAR, EVEN, ODD, OWN, PART, SHARE, WEIGHT, AUDIO = 0, 1, 2, 3, 4, 8, 12, 16


def table(shards, per_shard):
    rows = []
    for s in range(shards):
        y, x, z = place(s)
        step = 1 - 2 * (s % 2)
        for a in range(4):
            row = [(x + 2) % RING, x ^ 1, odd_swap(x, RING), x]
            row += [y ^ j ^ a for j in range(RING)] + [z ^ j for j in range(RING)]
            row += [a ^ j for j in range(4)]
            for shard in (s, s + step, s - step, s + 2 * step, s - 2 * step):
                row += [shard * per_shard + i for i in range(per_shard)]
            rows.append(row)
    return np.array(rows, np.int32)


def odd_swap(i, n):
    return (((i + 1) % n ^ 1) - 1) % n


def pick(array, i):
    return lax.dynamic_index_in_dim(array, i, 0, keepdims=False, allow_negative_indices=False)


def after(value, *earlier):
    return lax.optimization_barrier((value, *earlier))[0]


def add_half(own, got):
    return (own.astype(F32) + got.astype(F32)).astype(BF)


def local(video_query, audio_key, audio_value, window_first, window_count, out_weight, cotangent):
    tokens, feature = video_query.shape
    audio_rows = audio_key.shape[0]
    shards = lax.axis_size("vseq")
    device = lax.axis_index("vseq") * 4 + lax.axis_index("aseq")
    pos = pick(jnp.asarray(table(shards, audio_rows // ABLK)), device)
    each = range(shards)
    pa = [(i, i ^ 1) for i in each]
    pb = [(i, odd_swap(i, shards)) for i in each]

    def along(change):
        return [(i, index(*change(*place(i)))) for i in each]

    x_even = along(lambda y, x, z: (y, x ^ 1, z))
    x_odd = along(lambda y, x, z: (y, odd_swap(x, RING), z))
    y_even = along(lambda y, x, z: (y ^ 1, x, z))
    y_odd = along(lambda y, x, z: (odd_swap(y, RING), x, z))

    def exchange(send, even, odd):
        return lax.ppermute(send[0], "vseq", even), lax.ppermute(send[1], "vseq", odd)

    def direct(sends, change):
        return [
            lax.ppermute(send, "vseq", along(functools.partial(change, j + 1)))
            for j, send in enumerate(sends)
        ]

    key_block = pos[AUDIO:]
    first = jnp.repeat(window_first, VBLK)
    end = jnp.repeat(window_first + window_count, VBLK)
    allowed = (key_block[:, None] >= first[None, :]) & (key_block[:, None] < end[None, :])
    bias = jnp.where(allowed, 0.0, -1e30).astype(F32)

    weight_parts = out_weight.reshape(4, feature, feature)
    w0, w1, w2, w3 = [
        pick(weight_parts, pos[WEIGHT + j]) for j in range(4)
    ]
    w_core = jnp.concatenate([w3, w1], 0)
    cot_core = lax.ppermute(cotangent, "aseq", CORE)
    grad_near = dot(cot_core, w1, NN) + dot(cotangent, w0, NN)

    def halo(own, *first):
        by_a = lax.ppermute(own, "vseq", pa)
        by_b = lax.ppermute(own, "vseq", pb)
        by_a, by_b = after((by_a, by_b), *first)
        return own, by_a, by_b, lax.ppermute(by_b, "vseq", pa), lax.ppermute(by_a, "vseq", pb)

    keys = halo(after(audio_key, pos), bias)
    values = halo(audio_value, grad_near, w_core)

    cot_pair = lax.ppermute(after(cotangent, *keys[3:], *values[3:]), "aseq", PAIR)
    att, p, far_core, near, *near_far = forward_call(
        pos, video_query, keys, values, after(bias, grad_near, w2, w3), w_core, (cotangent, cot_core)
    )

    near_got = exchange(near_far, x_even, x_odd)
    cot_pair = after(cot_pair, *near_got)
    cot_both = lax.ppermute(cot_pair, "aseq", CORE)
    got_core = lax.ppermute(after(far_core, cot_pair), "aseq", CORE)
    near_send = beside(pos, near, near_got)
    near_got = exchange(near_send, x_even, x_odd)
    far_pair = (dot(after(att, *near_send), w2, NT) + got_core[:, :feature].astype(F32)).astype(BF)
    got_pair = lax.ppermute(far_pair, "aseq", PAIR)
    more, *more_far = weight_far(pos, cot_pair, after(cot_both, far_pair), att)
    more_got = exchange(more_far, x_even, x_odd)

    grad_query, g_own, g_a, g_b, g_aa, g_bb = backward_call(
        video_query, keys, values, p, att, grad_near, (cot_pair, after(cot_both, *more_far)), (w2, w3)
    )
    back_a = lax.ppermute(g_aa, "vseq", pa)
    back_b = lax.ppermute(g_bb, "vseq", pb)

    more_send = beside(pos, more, after(more_got, g_aa, g_bb, *near_got))
    more_got = exchange(more_send, x_even, x_odd)
    mixed_video = (
        dot(after(att, *more_send), w0, NT) + got_core[:, feature:].astype(F32) + got_pair.astype(F32)
    ).astype(BF)
    back_a, back_b = after((back_a, back_b), mixed_video)
    send_b = add_half(g_b, back_a)
    send_a = add_half(g_a, back_b)
    sum_b = lax.ppermute(send_b, "vseq", pb)
    sum_a = lax.ppermute(send_a, "vseq", pa)

    rows, *sends = rows_of(pos, near, near_got, more, after(more_got, send_a, send_b))
    y_got = exchange(sends, y_even, y_odd)
    y_got = exchange(pass_on(pos, rows, y_got), y_even, y_odd)
    grad_weight, *sends = plane_of(pos, rows, y_got)
    for got in direct(sends, lambda j, y, x, z: (y, x, z ^ j)):
        grad_weight = grad_weight + got.astype(F32)

    grad_key = g_own[0] + sum_a[0].astype(F32) + sum_b[0].astype(F32)
    grad_value = g_own[1] + sum_a[1].astype(F32) + sum_b[1].astype(F32)
    return mixed_video, grad_query, grad_key, grad_value, grad_weight


def solution(mesh):
    both = P("vseq", "aseq")
    in_specs = (both, both, both, P("vseq"), P("vseq"), P(None, "aseq"), both)
    return jax.shard_map(
        local, mesh=mesh, in_specs=in_specs, out_specs=(both,) * 5, check_vma=False
    )
```

```python
import functools
import math

import jax
import jax.numpy as jnp
import numpy as np
from jax import lax
from jax.experimental import pallas as pl
from jax.experimental.pallas import tpu as pltpu
from jax.sharding import PartitionSpec as P

HEAD = 128
VBLK = 128
ABLK = 32
RING = 4
PAIRED = 2
SCALE = 1.0 / math.sqrt(HEAD)
LOG2E = math.log2(math.e)
NT = (((1,), (1,)), ((), ()))
TN = (((0,), (0,)), ((), ()))
NN = (((1,), (0,)), ((), ()))
F32 = jnp.float32
BF = jnp.bfloat16
VMEM = 24 << 20
CORE = [(a, a ^ 1) for a in range(4)]
PAIR = [(a, a ^ 2) for a in range(4)]


def dot(a, b, dims):
    return lax.dot_general(a, b, dims, preferred_element_type=F32)


def attend_forward(
    pos, q_ref, k0, k1, k2, k3, k4, v0, v1, v2, v3, v4, bias_ref, w_ref, l0, l1,
    att_ref, p_ref, out_ref, gw_ref, far0, far1, all_ref,
):
    tokens = q_ref.shape[0]
    rows = k0.shape[0]
    blocks = rows // ABLK
    head = pl.program_id(0)
    for u in range(PAIRED):
        own = slice(u * HEAD, (u + 1) * HEAD)
        q = q_ref[:, own]
        scores = []
        for i, k in enumerate((k0, k1, k2, k3, k4)):
            tile = dot(k[:, own], q, NT).reshape(blocks, ABLK, tokens)
            tile = tile + bias_ref[blocks * i : blocks * (i + 1), :][:, None, :]
            scores.append(tile.reshape(rows, tokens))
        top = jnp.max(functools.reduce(jnp.maximum, scores), axis=0, keepdims=True)
        exponent = [jnp.exp2((tile - top) * (SCALE * LOG2E)) for tile in scores]
        total = jnp.sum(functools.reduce(jnp.add, exponent), axis=0, keepdims=True)
        share = 1.0 / total
        for i, tile in enumerate(exponent):
            p_ref[u, rows * i : rows * (i + 1), :] = (tile * share).astype(BF)
        values = jnp.concatenate([v[:, own] for v in (v0, v1, v2, v3, v4)], axis=0)
        att_ref[:, own] = dot(values, p_ref[u], TN).T.astype(BF)
    all_ref[:, pl.ds(pl.multiple_of(head * PAIRED * HEAD, PAIRED * HEAD), PAIRED * HEAD)] = att_ref[...]

    @pl.when(head == pl.num_programs(0) - 1)
    def _():
        out_ref[...] = dot(all_ref[...], w_ref[...], NT).astype(BF)
        weight_rows((l0, l1), all_ref, gw_ref)
        far0[...] = gw_ref[0, pos[FAR]]
        far1[...] = gw_ref[1, pos[FAR]]


def weight_rows(lefts, att_ref, gw_ref):
    part = gw_ref.shape[2]
    for j, left in enumerate(lefts):
        rows = dot(left[...], att_ref[...], TN).astype(BF)
        for i in range(RING):
            gw_ref[j, i] = rows[i * part : (i + 1) * part]


def attend_backward(
    q_ref, k0, k1, k2, k3, k4, v0, v1, v2, v3, v4, p_ref, att_ref, near_ref, c0, c1, w0, w1,
    dq_ref, g0, g1, g2, g3, g4,
):
    rows = k0.shape[0]
    wide = (near_ref[...] + dot(c0[...], w0[...], NN) + dot(c1[...], w1[...], NN)).astype(BF)
    for u in range(PAIRED):
        own = slice(u * HEAD, (u + 1) * HEAD)
        q = q_ref[:, own]
        do = wide[:, own]
        do_t = do.T
        delta = jnp.sum(
            do_t.astype(F32) * att_ref[:, own].T.astype(F32), axis=0, keepdims=True
        )
        values = jnp.concatenate([v[:, own] for v in (v0, v1, v2, v3, v4)], axis=0)
        keys = jnp.concatenate([k[:, own] for k in (k0, k1, k2, k3, k4)], axis=0)
        p = p_ref[u]
        ds = (p.astype(F32) * (dot(values, do_t, NN) - delta)).astype(BF)
        dk = dot(ds, q, NN) * SCALE
        dv = dot(p, do, NN)
        for i, out in enumerate((g0, g1, g2, g3, g4)):
            out[0, :, own] = dk[rows * i : rows * (i + 1)].astype(out.dtype)
            out[1, :, own] = dv[rows * i : rows * (i + 1)].astype(out.dtype)
        dq_ref[:, own] = (dot(keys, ds, TN) * SCALE).T


def call(kernel, grid, scalars, in_specs, out_specs, out_shape, scratch=(), name=None, cost=None):
    return pl.pallas_call(
        kernel,
        grid_spec=pltpu.PrefetchScalarGridSpec(
            num_scalar_prefetch=len(scalars),
            grid=grid,
            in_specs=in_specs,
            out_specs=out_specs,
            scratch_shapes=scratch,
        ),
        out_shape=out_shape,
        compiler_params=pltpu.CompilerParams(vmem_limit_bytes=VMEM),
        cost_estimate=cost,
        name=name,
    )


def whole(v):
    return pl.BlockSpec(v.shape, lambda *_: (0,) * len(v.shape))


def weight_far_kernel(pos, l0, l1, att_ref, gw_ref, far0, far1):
    weight_rows((l0, l1), att_ref, gw_ref)
    far0[...] = gw_ref[0, pos[FAR]]
    far1[...] = gw_ref[1, pos[FAR]]


def weight_far(pos, l0, l1, att):
    part, feature = l0.shape[1] // RING, att.shape[1]
    far = jax.ShapeDtypeStruct((part, feature), BF)
    shapes = [jax.ShapeDtypeStruct((2, RING, part, feature), BF), far, far]
    return call(
        weight_far_kernel,
        (1,),
        (pos,),
        [whole(l0), whole(l1), whole(att)],
        [whole(v) for v in shapes],
        shapes,
        name="weight_far",
    )(pos, l0, l1, att)


def beside_kernel(pos, even, odd, got_even, got_odd, to_even, to_odd):
    to_even[0] = even[0, 0]
    to_even[1] = (even[1, 0].astype(F32) + got_odd[...].astype(F32)).astype(BF)
    to_odd[0] = (odd[0, 0].astype(F32) + got_even[...].astype(F32)).astype(BF)
    to_odd[1] = odd[1, 0]


def beside(pos, chunks, got):
    _, _, part, feature = chunks.shape
    send = jax.ShapeDtypeStruct((2, part, feature), BF)
    pick = lambda k: pl.BlockSpec((2, 1, part, feature), lambda i, pos: (0, pos[k], 0, 0))
    return call(
        beside_kernel,
        (1,),
        (pos,),
        [pick(EVEN), pick(ODD), whole(got[0]), whole(got[1])],
        [whole(send)] * 2,
        [send] * 2,
        name="beside",
    )(pos, chunks, chunks, *got)


def rows_kernel(pos, near, near_even, near_odd, more, more_even, more_odd, rows, s_even, s_odd):
    for j, (own, even, odd) in enumerate(((near, near_even, near_odd), (more, more_even, more_odd))):
        total = own[:, 0].astype(F32) + even[...].astype(F32) + odd[...].astype(F32)
        rows[2 * j : 2 * j + 2] = total.astype(BF)
    half = s_even.shape[0]
    s_even[...] = rows[pos[PART + 2], :half]
    s_odd[...] = rows[pos[PART + 2], half:]


def rows_of(pos, near, near_got, more, more_got):
    _, _, part, feature = near.shape
    half = jax.ShapeDtypeStruct((part // 2, feature), BF)
    shapes = [jax.ShapeDtypeStruct((RING, part, feature), BF), half, half]
    own = pl.BlockSpec((2, 1, part, feature), lambda i, pos: (0, pos[OWN], 0, 0))
    got = whole(near_got[0])
    return call(
        rows_kernel,
        (1,),
        (pos,),
        [own, got, got] * 2,
        [whole(v) for v in shapes],
        shapes,
        name="rows",
    )(pos, near, *near_got, more, *more_got)


def pass_kernel(pos, rows, got_even, got_odd, to_even, to_odd):
    half = got_even.shape[0]
    to_even[:half] = rows[pos[PART + 1], :half]
    to_even[half:] = (rows[pos[PART + 1], half:].astype(F32) + got_odd[...].astype(F32)).astype(BF)
    to_odd[:half] = (rows[pos[PART + 3], :half].astype(F32) + got_even[...].astype(F32)).astype(BF)
    to_odd[half:] = rows[pos[PART + 3], half:]


def pass_on(pos, rows, got):
    send = jax.ShapeDtypeStruct(rows.shape[1:], BF)
    return call(
        pass_kernel,
        (1,),
        (pos,),
        [whole(v) for v in (rows, *got)],
        [whole(send)] * 2,
        [send] * 2,
        name="pass_on",
    )(pos, rows, *got)


def plane_kernel(pos, own, g1, g2, keep, s1, s2, s3, rows):
    each = own.shape[1] // RING
    total = own[pos[PART]].astype(F32) + g1[...].astype(F32) + g2[...].astype(F32)
    for i in range(RING):
        rows[i] = total[i * each : (i + 1) * each]
    keep[...] = rows[pos[SHARE]]
    for k, out in enumerate((s1, s2, s3)):
        out[...] = rows[pos[SHARE + 1 + k]].astype(BF)


def plane_of(pos, own, got):
    _, part, feature = own.shape
    each = part // RING
    shapes = [jax.ShapeDtypeStruct((each, feature), F32)] + [jax.ShapeDtypeStruct((each, feature), BF)] * 3
    return call(
        plane_kernel,
        (1,),
        (pos,),
        [whole(own)] + [whole(v) for v in got],
        [whole(v) for v in shapes],
        shapes,
        scratch=[pltpu.VMEM((RING, each, feature), F32)],
        name="plane",
    )(pos, own, *got)


def forward_call(pos, q, keys, values, bias, weight, lefts):
    tokens, feature = q.shape
    heads = feature // HEAD
    rows = keys[0].shape[0]
    band = rows * len(keys)
    part = feature // RING
    by_head = pl.BlockSpec((tokens, PAIRED * HEAD), lambda h, pos: (0, h))
    kv_head = pl.BlockSpec((rows, PAIRED * HEAD), lambda h, pos: (0, h))
    once = [
        jax.ShapeDtypeStruct((tokens, weight.shape[0]), BF),
        jax.ShapeDtypeStruct((2, RING, part, feature), BF),
        jax.ShapeDtypeStruct((part, feature), BF),
        jax.ShapeDtypeStruct((part, feature), BF),
    ]
    return call(
        attend_forward,
        (heads // PAIRED,),
        (pos,),
        [by_head] + [kv_head] * 10 + [whole(v) for v in (bias, weight, *lefts)],
        [by_head, pl.BlockSpec((PAIRED, band, tokens), lambda h, pos: (h, 0, 0))] + [whole(v) for v in once],
        [
            jax.ShapeDtypeStruct((tokens, feature), BF),
            jax.ShapeDtypeStruct((heads, band, tokens), BF),
        ]
        + once,
        scratch=[pltpu.VMEM((tokens, feature), BF)],
        name="attend_forward",
        cost=pl.CostEstimate(
            flops=8 * tokens * band * feature, bytes_accessed=0, transcendentals=heads * band * tokens
        ),
    )(pos, q, *keys, *values, bias, weight, *lefts)


def backward_call(q, keys, values, p, att, near, cots, weights):
    tokens, feature = q.shape
    heads = feature // HEAD
    rows = keys[0].shape[0]
    band = rows * len(keys)
    by_head = pl.BlockSpec((tokens, PAIRED * HEAD), lambda h: (0, h))
    kv_head = pl.BlockSpec((rows, PAIRED * HEAD), lambda h: (0, h))
    both_head = pl.BlockSpec((2, rows, PAIRED * HEAD), lambda h: (0, 0, h))
    piece = lambda kind: jax.ShapeDtypeStruct((2, rows, feature), kind)
    return call(
        attend_backward,
        (heads // PAIRED,),
        (),
        [by_head]
        + [kv_head] * 10
        + [pl.BlockSpec((PAIRED, band, tokens), lambda h: (h, 0, 0)), by_head, by_head]
        + [whole(v) for v in cots]
        + [pl.BlockSpec((feature, PAIRED * HEAD), lambda h: (0, h))] * len(weights),
        [by_head] + [both_head] * 5,
        [jax.ShapeDtypeStruct((tokens, feature), F32)]
        + [piece(F32), piece(F32), piece(F32), piece(BF), piece(BF)],
        name="attend_backward",
        cost=pl.CostEstimate(
            flops=12 * tokens * band * feature, bytes_accessed=0, transcendentals=0
        ),
    )(q, *keys, *values, p, att, near, *cots, *weights)


def place(s):
    return s // (RING * RING), (s // RING) % RING, s % RING


def index(y, x, z):
    return (y * RING + x) * RING + z


FAR, EVEN, ODD, OWN, PART, SHARE, WEIGHT, AUDIO = 0, 1, 2, 3, 4, 8, 12, 16


def table(shards, per_shard):
    rows = []
    for s in range(shards):
        y, x, z = place(s)
        step = 1 - 2 * (s % 2)
        for a in range(4):
            row = [(x + 2) % RING, x ^ 1, odd_swap(x, RING), x]
            row += [y ^ j ^ a for j in range(RING)] + [z ^ j for j in range(RING)]
            row += [a ^ j for j in range(4)]
            for shard in (s, s + step, s - step, s + 2 * step, s - 2 * step):
                row += [shard * per_shard + i for i in range(per_shard)]
            rows.append(row)
    return np.array(rows, np.int32)


def odd_swap(i, n):
    return (((i + 1) % n ^ 1) - 1) % n


def pick(array, i):
    return lax.dynamic_index_in_dim(array, i, 0, keepdims=False, allow_negative_indices=False)


def after(value, *earlier):
    return lax.optimization_barrier((value, *earlier))[0]


def add_half(own, got):
    return (own.astype(F32) + got.astype(F32)).astype(BF)


def local(video_query, audio_key, audio_value, window_first, window_count, out_weight, cotangent):
    tokens, feature = video_query.shape
    audio_rows = audio_key.shape[0]
    shards = lax.axis_size("vseq")
    device = lax.axis_index("vseq") * 4 + lax.axis_index("aseq")
    pos = pick(jnp.asarray(table(shards, audio_rows // ABLK)), device)
    each = range(shards)
    pa = [(i, i ^ 1) for i in each]
    pb = [(i, odd_swap(i, shards)) for i in each]

    def along(change):
        return [(i, index(*change(*place(i)))) for i in each]

    x_even = along(lambda y, x, z: (y, x ^ 1, z))
    x_odd = along(lambda y, x, z: (y, odd_swap(x, RING), z))
    y_even = along(lambda y, x, z: (y ^ 1, x, z))
    y_odd = along(lambda y, x, z: (odd_swap(y, RING), x, z))

    def exchange(send, even, odd):
        return lax.ppermute(send[0], "vseq", even), lax.ppermute(send[1], "vseq", odd)

    def direct(sends, change):
        return [
            lax.ppermute(send, "vseq", along(functools.partial(change, j + 1)))
            for j, send in enumerate(sends)
        ]

    key_block = pos[AUDIO:]
    first = jnp.repeat(window_first, VBLK)
    end = jnp.repeat(window_first + window_count, VBLK)
    allowed = (key_block[:, None] >= first[None, :]) & (key_block[:, None] < end[None, :])
    bias = jnp.where(allowed, 0.0, -1e30).astype(F32)

    weight_parts = out_weight.reshape(4, feature, feature)
    w0, w1, w2, w3 = [
        pick(weight_parts, pos[WEIGHT + j]) for j in range(4)
    ]
    w_core = jnp.concatenate([w3, w1], 0)
    cot_core = lax.ppermute(cotangent, "aseq", CORE)
    grad_near = dot(cot_core, w1, NN) + dot(cotangent, w0, NN)

    def halo(own, *first):
        by_a = lax.ppermute(own, "vseq", pa)
        by_b = lax.ppermute(own, "vseq", pb)
        by_a, by_b = after((by_a, by_b), *first)
        return own, by_a, by_b, lax.ppermute(by_b, "vseq", pa), lax.ppermute(by_a, "vseq", pb)

    keys = halo(after(audio_key, pos), bias)
    values = halo(audio_value, grad_near, w_core)

    cot_pair = lax.ppermute(after(cotangent, *keys[3:], *values[3:]), "aseq", PAIR)
    att, p, far_core, near, *near_far = forward_call(
        pos, video_query, keys, values, after(bias, grad_near, w2, w3), w_core, (cotangent, cot_core)
    )

    near_got = exchange(near_far, x_even, x_odd)
    cot_pair = after(cot_pair, *near_got)
    cot_both = lax.ppermute(cot_pair, "aseq", CORE)
    got_core = lax.ppermute(after(far_core, cot_pair), "aseq", CORE)
    near_send = beside(pos, near, near_got)
    near_got = exchange(near_send, x_even, x_odd)
    far_pair = (dot(after(att, *near_send), w2, NT) + got_core[:, :feature].astype(F32)).astype(BF)
    got_pair = lax.ppermute(far_pair, "aseq", PAIR)
    more, *more_far = weight_far(pos, cot_pair, after(cot_both, far_pair), att)
    more_got = exchange(more_far, x_even, x_odd)

    grad_query, g_own, g_a, g_b, g_aa, g_bb = backward_call(
        video_query, keys, values, p, att, grad_near, (cot_pair, after(cot_both, *more_far)), (w2, w3)
    )
    back_a = lax.ppermute(g_aa, "vseq", pa)
    back_b = lax.ppermute(g_bb, "vseq", pb)

    more_send = beside(pos, more, after(more_got, g_aa, g_bb, *near_got))
    more_got = exchange(more_send, x_even, x_odd)
    mixed_video = (
        dot(after(att, *more_send), w0, NT) + got_core[:, feature:].astype(F32) + got_pair.astype(F32)
    ).astype(BF)
    back_a, back_b = after((back_a, back_b), mixed_video)
    send_b = add_half(g_b, back_a)
    send_a = add_half(g_a, back_b)
    sum_b = lax.ppermute(send_b, "vseq", pb)
    sum_a = lax.ppermute(send_a, "vseq", pa)

    rows, *sends = rows_of(pos, near, near_got, more, after(more_got, send_a, send_b))
    y_got = exchange(sends, y_even, y_odd)
    y_got = exchange(pass_on(pos, rows, y_got), y_even, y_odd)
    grad_weight, *sends = plane_of(pos, rows, y_got)
    for got in direct(sends, lambda j, y, x, z: (y, x, z ^ j)):
        grad_weight = grad_weight + got.astype(F32)

    grad_key = g_own[0] + sum_a[0].astype(F32) + sum_b[0].astype(F32)
    grad_value = g_own[1] + sum_a[1].astype(F32) + sum_b[1].astype(F32)
    return mixed_video, grad_query, grad_key, grad_value, grad_weight


def solution(mesh):
    both = P("vseq", "aseq")
    in_specs = (both, both, both, P("vseq"), P("vseq"), P(None, "aseq"), both)
    return jax.shard_map(
        local, mesh=mesh, in_specs=in_specs, out_specs=(both,) * 5, check_vma=False
    )
```

```python
import functools
import math

import jax
import jax.numpy as jnp
import numpy as np
from jax import lax
from jax.experimental import pallas as pl
from jax.experimental.pallas import tpu as pltpu
from jax.sharding import PartitionSpec as P

HEAD = 128
VBLK = 128
ABLK = 32
RING = 4
PAIRED = 3
SCALE = 1.0 / math.sqrt(HEAD)
LOG2E = math.log2(math.e)
NT = (((1,), (1,)), ((), ()))
TN = (((0,), (0,)), ((), ()))
NN = (((1,), (0,)), ((), ()))
F32 = jnp.float32
BF = jnp.bfloat16
VMEM = 24 << 20
CORE = [(a, a ^ 1) for a in range(4)]
PAIR = [(a, a ^ 2) for a in range(4)]


def dot(a, b, dims):
    return lax.dot_general(a, b, dims, preferred_element_type=F32)


def attend_forward(
    pos, q_ref, k0, k1, k2, k3, k4, v0, v1, v2, v3, v4, bias_ref, w_ref, l0, l1,
    att_ref, p_ref, out_ref, gw_ref, far0, far1, all_ref,
):
    tokens = q_ref.shape[0]
    rows = k0.shape[0]
    blocks = rows // ABLK
    head = pl.program_id(0)
    for u in range(PAIRED):
        own = slice(u * HEAD, (u + 1) * HEAD)
        q = q_ref[:, own]
        scores = []
        for i, k in enumerate((k0, k1, k2, k3, k4)):
            tile = dot(k[:, own], q, NT).reshape(blocks, ABLK, tokens)
            tile = tile + bias_ref[blocks * i : blocks * (i + 1), :][:, None, :]
            scores.append(tile.reshape(rows, tokens))
        top = jnp.max(functools.reduce(jnp.maximum, scores), axis=0, keepdims=True)
        exponent = [jnp.exp2((tile - top) * (SCALE * LOG2E)) for tile in scores]
        total = jnp.sum(functools.reduce(jnp.add, exponent), axis=0, keepdims=True)
        share = 1.0 / total
        for i, tile in enumerate(exponent):
            p_ref[u, rows * i : rows * (i + 1), :] = (tile * share).astype(BF)
        values = jnp.concatenate([v[:, own] for v in (v0, v1, v2, v3, v4)], axis=0)
        att_ref[:, own] = dot(values, p_ref[u], TN).T.astype(BF)
    all_ref[:, pl.ds(pl.multiple_of(head * PAIRED * HEAD, PAIRED * HEAD), PAIRED * HEAD)] = att_ref[...]

    @pl.when(head == pl.num_programs(0) - 1)
    def _():
        out_ref[...] = dot(all_ref[...], w_ref[...], NT).astype(BF)
        weight_rows((l0, l1), all_ref, gw_ref)
        far0[...] = gw_ref[0, pos[FAR]]
        far1[...] = gw_ref[1, pos[FAR]]


def weight_rows(lefts, att_ref, gw_ref):
    part = gw_ref.shape[2]
    for j, left in enumerate(lefts):
        rows = dot(left[...], att_ref[...], TN).astype(BF)
        for i in range(RING):
            gw_ref[j, i] = rows[i * part : (i + 1) * part]


def attend_backward(
    q_ref, k0, k1, k2, k3, k4, v0, v1, v2, v3, v4, p_ref, att_ref, near_ref, c0, c1, w0, w1,
    dq_ref, g0, g1, g2, g3, g4, all_ref,
):
    head = pl.program_id(0)

    @pl.when(head == 0)
    def _():
        total = near_ref[...] + dot(c0[...], w0[...], NN) + dot(c1[...], w1[...], NN)
        all_ref[...] = total.astype(BF)

    grads = (g0, g1, g2, g3, g4)
    rows = k0.shape[0]
    wide = all_ref[:, pl.ds(pl.multiple_of(head * PAIRED * HEAD, PAIRED * HEAD), PAIRED * HEAD)]
    for u in range(PAIRED):
        own = slice(u * HEAD, (u + 1) * HEAD)
        q = q_ref[:, own]
        do = wide[:, own]
        do_t = do.T
        delta = jnp.sum(
            do_t.astype(F32) * att_ref[:, own].T.astype(F32), axis=0, keepdims=True
        )
        values = jnp.concatenate([v[:, own] for v in (v0, v1, v2, v3, v4)], axis=0)
        keys = jnp.concatenate([k[:, own] for k in (k0, k1, k2, k3, k4)], axis=0)
        p = p_ref[u]
        ds = (p.astype(F32) * (dot(values, do_t, NN) - delta)).astype(BF)
        dk = dot(ds, q, NN) * SCALE
        dv = dot(p, do, NN)
        for i, out in enumerate((g0, g1, g2, g3, g4)):
            out[0, :, own] = dk[rows * i : rows * (i + 1)].astype(out.dtype)
            out[1, :, own] = dv[rows * i : rows * (i + 1)].astype(out.dtype)
        dq_ref[:, own] = (dot(keys, ds, TN) * SCALE).T


def call(kernel, grid, scalars, in_specs, out_specs, out_shape, scratch=(), name=None, cost=None):
    return pl.pallas_call(
        kernel,
        grid_spec=pltpu.PrefetchScalarGridSpec(
            num_scalar_prefetch=len(scalars),
            grid=grid,
            in_specs=in_specs,
            out_specs=out_specs,
            scratch_shapes=scratch,
        ),
        out_shape=out_shape,
        compiler_params=pltpu.CompilerParams(vmem_limit_bytes=VMEM),
        cost_estimate=cost,
        name=name,
    )


def whole(v):
    return pl.BlockSpec(v.shape, lambda *_: (0,) * len(v.shape))


def weight_far_kernel(pos, l0, l1, att_ref, gw_ref, far0, far1):
    weight_rows((l0, l1), att_ref, gw_ref)
    far0[...] = gw_ref[0, pos[FAR]]
    far1[...] = gw_ref[1, pos[FAR]]


def weight_far(pos, l0, l1, att):
    part, feature = l0.shape[1] // RING, att.shape[1]
    far = jax.ShapeDtypeStruct((part, feature), BF)
    shapes = [jax.ShapeDtypeStruct((2, RING, part, feature), BF), far, far]
    return call(
        weight_far_kernel,
        (1,),
        (pos,),
        [whole(l0), whole(l1), whole(att)],
        [whole(v) for v in shapes],
        shapes,
        name="weight_far",
    )(pos, l0, l1, att)


def beside_kernel(pos, even, odd, got_even, got_odd, to_even, to_odd):
    to_even[0] = even[0, 0]
    to_even[1] = (even[1, 0].astype(F32) + got_odd[...].astype(F32)).astype(BF)
    to_odd[0] = (odd[0, 0].astype(F32) + got_even[...].astype(F32)).astype(BF)
    to_odd[1] = odd[1, 0]


def beside(pos, chunks, got):
    _, _, part, feature = chunks.shape
    send = jax.ShapeDtypeStruct((2, part, feature), BF)
    pick = lambda k: pl.BlockSpec((2, 1, part, feature), lambda i, pos: (0, pos[k], 0, 0))
    return call(
        beside_kernel,
        (1,),
        (pos,),
        [pick(EVEN), pick(ODD), whole(got[0]), whole(got[1])],
        [whole(send)] * 2,
        [send] * 2,
        name="beside",
    )(pos, chunks, chunks, *got)


def rows_kernel(pos, near, near_even, near_odd, more, more_even, more_odd, rows, s_even, s_odd):
    for j, (own, even, odd) in enumerate(((near, near_even, near_odd), (more, more_even, more_odd))):
        total = own[:, 0].astype(F32) + even[...].astype(F32) + odd[...].astype(F32)
        rows[2 * j : 2 * j + 2] = total.astype(BF)
    half = s_even.shape[0]
    s_even[...] = rows[pos[PART + 2], :half]
    s_odd[...] = rows[pos[PART + 2], half:]


def rows_of(pos, near, near_got, more, more_got):
    _, _, part, feature = near.shape
    half = jax.ShapeDtypeStruct((part // 2, feature), BF)
    shapes = [jax.ShapeDtypeStruct((RING, part, feature), BF), half, half]
    own = pl.BlockSpec((2, 1, part, feature), lambda i, pos: (0, pos[OWN], 0, 0))
    got = whole(near_got[0])
    return call(
        rows_kernel,
        (1,),
        (pos,),
        [own, got, got] * 2,
        [whole(v) for v in shapes],
        shapes,
        name="rows",
    )(pos, near, *near_got, more, *more_got)


def pass_kernel(pos, rows, got_even, got_odd, to_even, to_odd):
    half = got_even.shape[0]
    to_even[:half] = rows[pos[PART + 1], :half]
    to_even[half:] = (rows[pos[PART + 1], half:].astype(F32) + got_odd[...].astype(F32)).astype(BF)
    to_odd[:half] = (rows[pos[PART + 3], :half].astype(F32) + got_even[...].astype(F32)).astype(BF)
    to_odd[half:] = rows[pos[PART + 3], half:]


def pass_on(pos, rows, got):
    send = jax.ShapeDtypeStruct(rows.shape[1:], BF)
    return call(
        pass_kernel,
        (1,),
        (pos,),
        [whole(v) for v in (rows, *got)],
        [whole(send)] * 2,
        [send] * 2,
        name="pass_on",
    )(pos, rows, *got)


def plane_kernel(pos, own, g1, g2, keep, s1, s2, s3, rows):
    each = own.shape[1] // RING
    total = own[pos[PART]].astype(F32) + g1[...].astype(F32) + g2[...].astype(F32)
    for i in range(RING):
        rows[i] = total[i * each : (i + 1) * each]
    keep[...] = rows[pos[SHARE]]
    for k, out in enumerate((s1, s2, s3)):
        out[...] = rows[pos[SHARE + 1 + k]].astype(BF)


def plane_of(pos, own, got):
    _, part, feature = own.shape
    each = part // RING
    shapes = [jax.ShapeDtypeStruct((each, feature), F32)] + [jax.ShapeDtypeStruct((each, feature), BF)] * 3
    return call(
        plane_kernel,
        (1,),
        (pos,),
        [whole(own)] + [whole(v) for v in got],
        [whole(v) for v in shapes],
        shapes,
        scratch=[pltpu.VMEM((RING, each, feature), F32)],
        name="plane",
    )(pos, own, *got)


def forward_call(pos, q, keys, values, bias, weight, lefts):
    tokens, feature = q.shape
    heads = feature // HEAD
    rows = keys[0].shape[0]
    band = rows * len(keys)
    part = feature // RING
    by_head = pl.BlockSpec((tokens, PAIRED * HEAD), lambda h, pos: (0, h))
    kv_head = pl.BlockSpec((rows, PAIRED * HEAD), lambda h, pos: (0, h))
    once = [
        jax.ShapeDtypeStruct((tokens, weight.shape[0]), BF),
        jax.ShapeDtypeStruct((2, RING, part, feature), BF),
        jax.ShapeDtypeStruct((part, feature), BF),
        jax.ShapeDtypeStruct((part, feature), BF),
    ]
    return call(
        attend_forward,
        (heads // PAIRED,),
        (pos,),
        [by_head] + [kv_head] * 10 + [whole(v) for v in (bias, weight, *lefts)],
        [by_head, pl.BlockSpec((PAIRED, band, tokens), lambda h, pos: (h, 0, 0))] + [whole(v) for v in once],
        [
            jax.ShapeDtypeStruct((tokens, feature), BF),
            jax.ShapeDtypeStruct((heads, band, tokens), BF),
        ]
        + once,
        scratch=[pltpu.VMEM((tokens, feature), BF)],
        name="attend_forward",
        cost=pl.CostEstimate(
            flops=8 * tokens * band * feature, bytes_accessed=0, transcendentals=heads * band * tokens
        ),
    )(pos, q, *keys, *values, bias, weight, *lefts)


def backward_call(q, keys, values, p, att, near, cots, weights):
    tokens, feature = q.shape
    heads = feature // HEAD
    rows = keys[0].shape[0]
    band = rows * len(keys)
    by_head = pl.BlockSpec((tokens, PAIRED * HEAD), lambda h: (0, h))
    kv_head = pl.BlockSpec((rows, PAIRED * HEAD), lambda h: (0, h))
    both_head = pl.BlockSpec((2, rows, PAIRED * HEAD), lambda h: (0, 0, h))
    piece = lambda kind: jax.ShapeDtypeStruct((2, rows, feature), kind)
    return call(
        attend_backward,
        (heads // PAIRED,),
        (),
        [by_head]
        + [kv_head] * 10
        + [pl.BlockSpec((PAIRED, band, tokens), lambda h: (h, 0, 0)), by_head]
        + [whole(v) for v in (near, *cots, *weights)],
        [by_head] + [both_head] * 5,
        [jax.ShapeDtypeStruct((tokens, feature), F32)]
        + [piece(F32), piece(F32), piece(F32), piece(BF), piece(BF)],
        scratch=[pltpu.VMEM((tokens, feature), BF)],
        name="attend_backward",
        cost=pl.CostEstimate(
            flops=12 * tokens * band * feature, bytes_accessed=0, transcendentals=0
        ),
    )(q, *keys, *values, p, att, near, *cots, *weights)


def place(s):
    return s // (RING * RING), (s // RING) % RING, s % RING


def index(y, x, z):
    return (y * RING + x) * RING + z


FAR, EVEN, ODD, OWN, PART, SHARE, WEIGHT, AUDIO = 0, 1, 2, 3, 4, 8, 12, 16


def table(shards, per_shard):
    rows = []
    for s in range(shards):
        y, x, z = place(s)
        step = 1 - 2 * (s % 2)
        for a in range(4):
            row = [(x + 2) % RING, x ^ 1, odd_swap(x, RING), x]
            row += [y ^ j ^ a for j in range(RING)] + [z ^ j for j in range(RING)]
            row += [a ^ j for j in range(4)]
            for shard in (s, s + step, s - step, s + 2 * step, s - 2 * step):
                row += [shard * per_shard + i for i in range(per_shard)]
            rows.append(row)
    return np.array(rows, np.int32)


def odd_swap(i, n):
    return (((i + 1) % n ^ 1) - 1) % n


def pick(array, i):
    return lax.dynamic_index_in_dim(array, i, 0, keepdims=False, allow_negative_indices=False)


def after(value, *earlier):
    return lax.optimization_barrier((value, *earlier))[0]


def add_half(own, got):
    return (own.astype(F32) + got.astype(F32)).astype(BF)


def local(video_query, audio_key, audio_value, window_first, window_count, out_weight, cotangent):
    tokens, feature = video_query.shape
    audio_rows = audio_key.shape[0]
    shards = lax.axis_size("vseq")
    device = lax.axis_index("vseq") * 4 + lax.axis_index("aseq")
    pos = pick(jnp.asarray(table(shards, audio_rows // ABLK)), device)
    each = range(shards)
    pa = [(i, i ^ 1) for i in each]
    pb = [(i, odd_swap(i, shards)) for i in each]

    def along(change):
        return [(i, index(*change(*place(i)))) for i in each]

    x_even = along(lambda y, x, z: (y, x ^ 1, z))
    x_odd = along(lambda y, x, z: (y, odd_swap(x, RING), z))
    y_even = along(lambda y, x, z: (y ^ 1, x, z))
    y_odd = along(lambda y, x, z: (odd_swap(y, RING), x, z))

    def exchange(send, even, odd):
        return lax.ppermute(send[0], "vseq", even), lax.ppermute(send[1], "vseq", odd)

    def direct(sends, change):
        return [
            lax.ppermute(send, "vseq", along(functools.partial(change, j + 1)))
            for j, send in enumerate(sends)
        ]

    key_block = pos[AUDIO:]
    first = jnp.repeat(window_first, VBLK)
    end = jnp.repeat(window_first + window_count, VBLK)
    allowed = (key_block[:, None] >= first[None, :]) & (key_block[:, None] < end[None, :])
    bias = jnp.where(allowed, 0.0, -1e30).astype(F32)

    weight_parts = out_weight.reshape(4, feature, feature)
    w0, w1, w2, w3 = [
        pick(weight_parts, pos[WEIGHT + j]) for j in range(4)
    ]
    w_core = jnp.concatenate([w3, w1], 0)
    cot_core = lax.ppermute(cotangent, "aseq", CORE)
    grad_near = dot(cot_core, w1, NN) + dot(cotangent, w0, NN)

    def halo(own, *first):
        by_a = lax.ppermute(own, "vseq", pa)
        by_b = lax.ppermute(own, "vseq", pb)
        by_a, by_b = after((by_a, by_b), *first)
        return own, by_a, by_b, lax.ppermute(by_b, "vseq", pa), lax.ppermute(by_a, "vseq", pb)

    keys = halo(after(audio_key, pos), bias)
    values = halo(audio_value, grad_near, w_core)

    cot_pair = lax.ppermute(after(cotangent, *keys[3:], *values[3:]), "aseq", PAIR)
    att, p, far_core, near, *near_far = forward_call(
        pos, video_query, keys, values, after(bias, grad_near, w2, w3), w_core, (cotangent, cot_core)
    )

    near_got = exchange(near_far, x_even, x_odd)
    cot_pair = after(cot_pair, *near_got)
    cot_both = lax.ppermute(cot_pair, "aseq", CORE)
    got_core = lax.ppermute(after(far_core, cot_pair), "aseq", CORE)
    near_send = beside(pos, near, near_got)
    near_got = exchange(near_send, x_even, x_odd)
    far_pair = (dot(after(att, *near_send), w2, NT) + got_core[:, :feature].astype(F32)).astype(BF)
    got_pair = lax.ppermute(far_pair, "aseq", PAIR)
    more, *more_far = weight_far(pos, cot_pair, after(cot_both, far_pair), att)
    more_got = exchange(more_far, x_even, x_odd)

    grad_query, g_own, g_a, g_b, g_aa, g_bb = backward_call(
        video_query, keys, values, p, att, grad_near, (cot_pair, after(cot_both, *more_far)), (w2, w3)
    )
    back_a = lax.ppermute(g_aa, "vseq", pa)
    back_b = lax.ppermute(g_bb, "vseq", pb)

    more_send = beside(pos, more, after(more_got, g_aa, g_bb, *near_got))
    more_got = exchange(more_send, x_even, x_odd)
    mixed_video = (
        dot(after(att, *more_send), w0, NT) + got_core[:, feature:].astype(F32) + got_pair.astype(F32)
    ).astype(BF)
    back_a, back_b = after((back_a, back_b), mixed_video)
    send_b = add_half(g_b, back_a)
    send_a = add_half(g_a, back_b)
    sum_b = lax.ppermute(send_b, "vseq", pb)
    sum_a = lax.ppermute(send_a, "vseq", pa)

    rows, *sends = rows_of(pos, near, near_got, more, after(more_got, send_a, send_b))
    y_got = exchange(sends, y_even, y_odd)
    y_got = exchange(pass_on(pos, rows, y_got), y_even, y_odd)
    grad_weight, *sends = plane_of(pos, rows, y_got)
    for got in direct(sends, lambda j, y, x, z: (y, x, z ^ j)):
        grad_weight = grad_weight + got.astype(F32)

    grad_key = g_own[0] + sum_a[0].astype(F32) + sum_b[0].astype(F32)
    grad_value = g_own[1] + sum_a[1].astype(F32) + sum_b[1].astype(F32)
    return mixed_video, grad_query, grad_key, grad_value, grad_weight


def solution(mesh):
    both = P("vseq", "aseq")
    in_specs = (both, both, both, P("vseq"), P("vseq"), P(None, "aseq"), both)
    return jax.shard_map(
        local, mesh=mesh, in_specs=in_specs, out_specs=(both,) * 5, check_vma=False
    )
```
